1024 devices in a mesh: wave: 64 (over z, y), lev: 16 (over x, core).
Axes of the slice: x: 8, y: 8, z: 8, core: 2. Of those that a mesh axis runs over, the one named last changes fastest.
Arguments:
- spectra: bfloat16 [640, 3, 96, 2, 640], P('wave', None, 'lev'), may hold values from -0.3125 to 0.3125
- vertical: bfloat16 [3, 96, 96], replicated, may hold values from -0.625 to 0.625
- legendre: bfloat16 [640, 64, 640], P('wave'), may hold values from -0.25 to 0.25
- tile_mask: int32 [640, 10, 1], P('wave'), may hold values from 0 to 1, as said below
- assign: int32 [640], replicated, may hold values from 0 to 639, as said below
- row_points: int32 [64], P('wave'), may hold values from 20 to 2576, as said below
- quadrature: float32 [64], P('wave'), may hold values from 10 to 100
- forcing: bfloat16 [3, 96, 2, 64, 2688], P(None, 'lev', None, 'wave'), may hold values from -6 to 6
Outputs:
- grid_field: bfloat16 [3, 96, 2, 64, 2688], P(None, 'lev', None, 'wave')
- spectra_out: bfloat16 [640, 3, 96, 2, 640], P('wave', None, 'lev')
The draws below stay inside these ranges and needn't reach their ends.
Inputs may be any that keep to these rules, and one draw needn't show every extreme that they name: `assign`: every zonal wavenumber is held by exactly one slot; the slots of one wave index are consecutive. tile_mask[s, b, r] = 1 marks a nonzero Legendre tile of slot s: total wavenumbers b * 64 to (b + 1) * 64 - 1, north rows r * 64 to (r + 1) * 64 - 1. A tile is marked only if it holds some total wavenumber at or above the slot's zonal wavenumber. row_points[h] = 20 + 4 i, with i the octahedral index of north row h counted from the pole; i rises strictly with h, and the last north row is the one next to the equator, with 2576 points.
All inputs are finite; a program needn't handle non-finite values.
Results may differ from the reference program's by a relative error of at most 0.0085.
Values may be sent and summed in bfloat16 or wider, within the bound.
A program may use at most 64 MiB of HBM per device.

```python
import math
import jax
import jax.numpy as jnp
from jax import lax

NT = 640
MW = 640
NTILE = 64
FIELDS = 3
LEV = 96
LATH = 64
LTILE = 64
PSTORE = 2688


def wave_order(key):
    return jax.random.permutation(key, MW).astype(jnp.int32)


def draw_assign(key, part):
    return wave_order(key)


def draw_tile_mask(key, part):
    waves_held = wave_order(key)
    key = jax.random.fold_in(key, 5)
    north_tiles = LATH // LTILE
    ceiling = waves_held * north_tiles // MW + 1
    dropped = jax.random.randint(key, (MW,), 0, ceiling).astype(jnp.int32)
    degree_blocks = jnp.arange(NT // NTILE, dtype=jnp.int32)
    north_index = jnp.arange(north_tiles, dtype=jnp.int32)
    reaches_wave = NTILE * (degree_blocks[None, :, None] + 1) > waves_held[:, None, None]
    beyond_cut = north_index[None, None, :] >= dropped[:, None, None]
    return (reaches_wave & beyond_cut).astype(jnp.int32)


def draw_row_points(key, part):
    key = jax.random.fold_in(key, 9)
    chosen = jax.random.permutation(key, NT - 1)[:LATH - 1]
    ordered = jnp.sort(chosen).astype(jnp.int32)
    indices = jnp.concatenate([ordered, jnp.full((1,), NT - 1, jnp.int32)])
    return (20 + 4 * indices).astype(jnp.int32)


def levels(key, shape, cuts, smallest, top_value):
    def one(axis_at, parts):
        draws = jax.random.uniform(jax.random.fold_in(jax.random.fold_in(key, 6), axis_at), (parts,), jnp.float32, smallest / len(cuts), top_value / len(cuts))
        return jnp.repeat(jnp.exp(draws), shape[axis_at] // parts).reshape((-1,) + (1,) * (len(shape) - axis_at - 1))

    gain = one(*cuts[0])
    for cut in cuts[1:]:
        gain = gain * one(*cut)
    return gain


def scatter_about(key, extent, spread, bound, split=(), kind=jnp.bfloat16):
    values = jax.random.normal(key, extent, jnp.float32) * spread
    if len(split) > 0:
        values = levels(key, extent, split, -0.22, 0.18) * values
    return jnp.clip(values, min=-bound, max=bound).astype(kind)


def setup_inputs(seed: int = 0) -> dict:
    streams_of = jax.random.split(jax.random.key(seed), 9)
    return {
        "spectra": scatter_about(streams_of[0], (MW, FIELDS, LEV, 2, NT), 0.05, 0.3125, ((0, 64), (2, 16))),
        "vertical": scatter_about(streams_of[1], (FIELDS, LEV, LEV), LEV ** -0.5, 0.625),
        "legendre": scatter_about(streams_of[2], (MW, LATH, NT), NT ** -0.5, 0.25, ((0, 64),)),
        "tile_mask": draw_tile_mask(jax.random.fold_in(streams_of[8], 71), 0),
        "assign": draw_assign(jax.random.fold_in(streams_of[8], 71), 0),
        "row_points": draw_row_points(jax.random.fold_in(streams_of[8], 71), 0),
        "quadrature": jnp.clip(jnp.exp(math.log(100.0) - 2.3025851 * jax.random.uniform(streams_of[6], (LATH,), jnp.float32) ** levels(streams_of[6], (LATH,), ((0, 64),), -0.2, 0.2)), 10.0, 100.0),
        "forcing": scatter_about(streams_of[7], (FIELDS, LEV, 2, LATH, PSTORE), 1.0, 6.0, ((1, 16), (3, 64))),
    }


def phase_table(wave_numbers, row_length, first_point, point_count):
    column = first_point + lax.broadcasted_iota(jnp.int32, (wave_numbers.shape[0], point_count), 1)
    remainder = (wave_numbers[:, None] * column) % row_length
    angles = remainder.astype(jnp.float32) * (2.0 * math.pi / row_length.astype(jnp.float32))
    usable = (column < row_length) & (2 * wave_numbers[:, None] < row_length)
    cosine = jnp.where(usable, jnp.cos(angles), jnp.float32(0.0))
    minus_sine = jnp.where(usable, -jnp.sin(angles), jnp.float32(0.0))
    return jnp.stack([cosine, minus_sine]).astype(jnp.bfloat16)


def live_block(legendre_slot, tiles_slot, wave_number):
    tile_rows = legendre_slot.shape[0] // tiles_slot.shape[0]
    tile_cols = legendre_slot.shape[1] // tiles_slot.shape[1]
    expanded = jnp.repeat(jnp.repeat(tiles_slot, tile_rows, axis=0), tile_cols, axis=1)
    degree = lax.broadcasted_iota(jnp.int32, legendre_slot.shape, 0)
    kept_mask = (expanded > 0) & (degree >= wave_number)
    return jnp.where(kept_mask, legendre_slot, jnp.zeros_like(legendre_slot))


def hemisphere_signs(wave_number):
    degree = jnp.arange(NT, dtype=jnp.int32)
    south = jnp.where((degree - wave_number) % 2 == 0, 1.0, -1.0)
    return jnp.stack([jnp.ones_like(south), south]).astype(jnp.float32)


def reference(spectra, vertical, legendre, tile_mask, assign, row_points, quadrature, forcing):
    vertical_wide = vertical.astype(jnp.float32)

    def inverse_slot(slot_inputs):
        spectra_slot, legendre_slot, tiles_slot, wave_number = slot_inputs
        coupled = jnp.einsum('fab,fbrn->farn', vertical_wide, spectra_slot.astype(jnp.float32)).astype(jnp.bfloat16)
        live = live_block(legendre_slot.T, tiles_slot, wave_number).astype(jnp.float32)
        signs = hemisphere_signs(wave_number)
        fourier = jnp.einsum('farn,en,nh->hfaer', coupled.astype(jnp.float32), signs, live)
        return fourier.astype(jnp.bfloat16)

    fourier = lax.map(inverse_slot, (spectra, legendre, tile_mask, assign))
    by_rows = jnp.transpose(fourier, (1, 2, 3, 4, 5, 0))
    forcing_rows = jnp.transpose(forcing, (3, 0, 1, 2, 4))
    factors = jnp.where(assign == 0, 1.0, 2.0).astype(jnp.float32)
    channels = FIELDS * LEV * 2

    def row_transform(row_inputs):
        fourier_row, forcing_row, row_length, weight = row_inputs
        phase_rows = phase_table(assign, row_length, 0, PSTORE).astype(jnp.float32).reshape(2 * MW, PSTORE)
        scaled = (fourier_row.astype(jnp.float32) * factors).reshape(channels, 2 * MW)
        grid_row = jnp.dot(scaled, phase_rows, precision=lax.Precision.HIGHEST).astype(jnp.bfloat16)
        summed = (grid_row.astype(jnp.float32) + forcing_row.reshape(channels, PSTORE).astype(jnp.float32)).astype(jnp.bfloat16)
        fourier_back = jnp.dot(summed.astype(jnp.float32), phase_rows.T, precision=lax.Precision.HIGHEST)
        row_scale = weight / row_length.astype(jnp.float32)
        weighted = (fourier_back * row_scale).astype(jnp.bfloat16)
        return grid_row.reshape(FIELDS, LEV, 2, PSTORE), weighted.reshape(FIELDS, LEV, 2, 2, MW)

    grid_rows, weighted = lax.map(row_transform, (by_rows, forcing_rows, row_points, quadrature))
    grid_field = jnp.transpose(grid_rows, (1, 2, 3, 0, 4))
    by_slots = jnp.transpose(weighted, (5, 0, 1, 2, 3, 4))

    def direct_slot(slot_inputs):
        weighted_slot, legendre_slot, tiles_slot, wave_number = slot_inputs
        live = live_block(legendre_slot.T, tiles_slot, wave_number).astype(jnp.float32)
        signs = hemisphere_signs(wave_number)
        result = jnp.einsum('hfaer,en,nh->farn', weighted_slot.astype(jnp.float32), signs, live)
        return result.astype(jnp.bfloat16)

    spectra_out = lax.map(direct_slot, (by_slots, legendre, tile_mask, assign))
    return grid_field, spectra_out
```

```python
import functools
import math

import jax
import jax.numpy as jnp
from jax import lax
from jax.experimental import pallas as pl
from jax.experimental.pallas import tpu as pltpu
from jax.sharding import PartitionSpec as P

MESH = pl.DeviceIdType.MESH
F32 = jnp.float32
BF16 = jnp.bfloat16
LANES = 128
FIELDS = 3
OWN_LEVELS = 6
SLOTS = 10
GROUPS = 4
THIRDS = 3
PITCH = 40
LEVEL_PITCH = 24
ROWS = 2 * GROUPS
CHANNELS = 2 * FIELDS * OWN_LEVELS
NT_DIMS = (((1,), (1,)), ((), ()))


def cosine_of_turns(turns):
    angle = (turns - jnp.round(turns)) * F32(2.0 * math.pi)
    square = angle * angle
    total = jnp.full_like(square, (-1.0) ** 9 / math.factorial(18))
    for k in range(8, -1, -1):
        total = total * square + F32((-1.0) ** k / math.factorial(2 * k))
    return total


def turns_of(product, length, inverse):
    return (product - jnp.floor(product * inverse) * length) * inverse


def slots_of():
    return [(s, s // GROUPS, s % GROUPS) for s in range(SLOTS)]


def kernel(
    waves,
    levs,
    spectra,
    legendre,
    tiles,
    assign,
    row_points,
    quadrature,
    vertical,
    forcing,
    grid_out,
    spectra_out,
    weights,
    mixer,
    phase,
    plane,
    rows32,
    turned,
    spread,
    channels,
    summed,
    send_a,
    recv_a,
    send_b,
    recv_b,
    send_c,
    recv_c,
    send_sems,
    recv_sems,
):
    wave = lax.axis_index("wave")
    lev = lax.axis_index("lev")
    own_rows = waves // levs
    part = own_rows * ROWS
    total_rows = waves * ROWS
    degrees = spectra.shape[2]
    points = forcing.shape[1]

    barrier = pltpu.get_barrier_semaphore()

    def greet_lev(k, carry):
        pl.semaphore_signal(
            barrier, inc=1, device_id=(wave, lax.rem(lev + k, levs)), device_id_type=MESH
        )
        return carry

    def greet_wave(k, carry):
        pl.semaphore_signal(
            barrier, inc=1, device_id=(lax.rem(wave + k, waves), lev), device_id_type=MESH
        )
        return carry

    lax.fori_loop(1, levs, greet_lev, 0)
    lax.fori_loop(1, waves, greet_wave, 0)

    turned[...] = jnp.zeros_like(turned)
    plane[...] = jnp.zeros_like(plane)
    degree = lax.broadcasted_iota(jnp.int32, (1, degrees), 1)
    lane = lax.broadcasted_iota(jnp.int32, (1, LANES), 1)
    half = degrees // (2 * LANES // 2)
    for s, third, group in slots_of():
        wave_number = assign[wave * SLOTS + s]
        marks = jnp.concatenate(
            [
                jnp.where(lane < LANES // 2, tiles[s, 2 * k], tiles[s, 2 * k + 1])
                for k in range(half)
            ],
            axis=1,
        )
        offset = degree - wave_number
        live = jnp.where((marks > 0) & (offset >= 0), F32(1.0), F32(0.0))
        signed = jnp.where((offset & 1) == 0, live, -live)
        table = legendre[s].astype(F32)
        lath = table.shape[0]
        weights[s, 0:lath, :] = (table * live).astype(BF16)
        weights[s, lath : 2 * lath, :] = (table * signed).astype(BF16)
        factor = jnp.where(wave_number == 0, F32(1.0), F32(2.0))
        plane[0:CHANNELS, 0 : 2 * lath] = factor * lax.dot_general(
            spectra[s], weights[s], NT_DIMS, preferred_element_type=F32
        )
        for part_at in range(2):
            block = plane[pl.ds(part_at, PITCH // 2, stride=2), :]
            row = group * 2 + part_at
            base = row * LANES + third * PITCH
            turned[pl.ds(base, PITCH // 2, stride=2), :] = block
            turned[pl.ds(base + 1, PITCH // 2, stride=2), :] = pltpu.roll(
                block, LANES - lath, axis=1
            )
    for row in range(ROWS):
        flipped = turned[row * LANES : (row + 1) * LANES, :].T
        spread[pl.ds(row, waves, stride=ROWS), :] = flipped[0:waves, :]
    send_a[...] = spread[0:total_rows, :].astype(BF16)

    pl.semaphore_wait(barrier, levs - 1 + waves - 1)

    def copy_a(target):
        return pltpu.make_async_remote_copy(
            src_ref=send_a.at[pl.ds(pl.multiple_of(target * part, part), part), :],
            dst_ref=recv_a.at[lev],
            send_sem=send_sems.at[0],
            recv_sem=recv_sems.at[0],
            device_id=(wave, target),
            device_id_type=MESH,
        )

    def start_a(k, carry):
        copy_a(lax.rem(lev + k, levs)).start()
        return carry

    lax.fori_loop(1, levs, start_a, 0)
    own_a = pltpu.make_async_copy(
        send_a.at[pl.ds(pl.multiple_of(lev * part, part), part), :],
        recv_a.at[lev],
        recv_sems.at[0],
    )
    own_a.start()

    levels = vertical.shape[1]
    edge = levs * LEVEL_PITCH
    at_row = lax.broadcasted_iota(jnp.int32, (edge, levels), 0)
    at_level = lax.broadcasted_iota(jnp.int32, (edge, levels), 1)
    at_group = (at_row * 2731) >> 16
    at_inner = at_row - at_group * LEVEL_PITCH
    at_field = (at_inner * 43) >> 8
    wanted = at_group * OWN_LEVELS + at_inner - at_field * OWN_LEVELS
    mixed = jnp.zeros((edge, edge), F32)
    for field in range(FIELDS):
        pick = jnp.where((at_field == field) & (at_level == wanted), F32(1.0), F32(0.0)).astype(
            BF16
        )
        rows = jnp.dot(pick, vertical[field], preferred_element_type=F32).astype(BF16)
        mixed = mixed + lax.dot_general(rows, pick, NT_DIMS, preferred_element_type=F32)
    mixer[...] = mixed.astype(BF16)

    length = row_points[0]
    length_f = length.astype(F32)
    inverse = F32(1.0) / length_f
    fine = THIRDS * 2 * ROWS
    at = lax.broadcasted_iota(jnp.int32, (2 * ROWS, LANES), 0)
    at_pair = at >> 1
    quarter = (at & 1).astype(F32) * F32(0.25)
    column = lax.broadcasted_iota(jnp.int32, (2 * ROWS, LANES), 1).astype(F32)

    def phase_rows(step, carry):
        numbers = []
        for third in range(THIRDS):
            number = jnp.zeros((2 * ROWS, LANES), jnp.int32)
            for pair in range(2):
                for group in range(GROUPS):
                    s = third * GROUPS + group
                    if s < SLOTS:
                        held = assign[(step * 2 + pair) * SLOTS + s]
                        number = jnp.where(at_pair == pair * GROUPS + group, held, number)
            numbers.append(number)
        number = jnp.concatenate(numbers, axis=0)
        real = [[s < SLOTS for s in range(t * GROUPS, (t + 1) * GROUPS)] for t in range(THIRDS)]
        usable = 2 * number < length
        group_at = at_pair & (GROUPS - 1)
        kept = jnp.concatenate(
            [jnp.where(group_at < sum(real[t]), F32(1.0), F32(0.0)) for t in range(THIRDS)], axis=0
        )
        kept = jnp.where(usable, kept, F32(0.0))
        number = number.astype(F32)
        columns = jnp.concatenate([column] * THIRDS, axis=0)
        quarters = jnp.concatenate([quarter] * THIRDS, axis=0)
        before = kept * cosine_of_turns(turns_of(number * columns, length_f, inverse) + quarters)
        now = kept * cosine_of_turns(
            turns_of(number * (columns + F32(LANES)), length_f, inverse) + quarters
        )
        twice = F32(2.0) * cosine_of_turns(turns_of(number * F32(LANES), length_f, inverse))
        for block in range(points // LANES):
            value = before.astype(BF16)
            for third in range(THIRDS):
                phase[
                    pl.ds(pl.multiple_of(third * total_rows + step * 2 * ROWS, 2 * ROWS), 2 * ROWS),
                    block * LANES : (block + 1) * LANES,
                ] = value[third * 2 * ROWS : (third + 1) * 2 * ROWS, :]
            before, now = now, twice * now - before
        return carry

    lax.fori_loop(0, waves // 2, phase_rows, 0)

    whole_a = pltpu.make_async_copy(recv_a, recv_a, recv_sems.at[0])
    whole_a.wait()
    for source in range(levs):
        rows32[source * LANES : (source + 1) * LANES, 0:part] = recv_a[source].astype(F32).T
    for third in range(THIRDS):
        for side in range(2):
            start = third * PITCH + side
            block = jnp.concatenate(
                [
                    rows32[pl.ds(source * LANES + start, LEVEL_PITCH, stride=2), :]
                    for source in range(levs)
                ],
                axis=0,
            ).astype(BF16)
            product = jnp.dot(mixer[...], block, preferred_element_type=F32)
            for target in range(levs):
                turned[pl.ds(target * LANES + start, PITCH // 2, stride=2), :] = product[
                    target * LEVEL_PITCH : target * LEVEL_PITCH + PITCH // 2, :
                ]
    for target in range(levs):
        flipped = turned[target * LANES : (target + 1) * LANES, :].T[0:part, :]
        send_b[target] = flipped.astype(BF16).reshape(own_rows, ROWS, LANES)

    def place_b(k):
        turn = lax.rem(k + wave + lev, waves)
        target = turn // own_rows
        row = lax.rem(turn, own_rows)
        return row, target, (lev * own_rows + row == wave) & (target == lev)

    def copy_b(row, target):
        return pltpu.make_async_remote_copy(
            src_ref=send_b.at[target, row],
            dst_ref=recv_b.at[wave],
            send_sem=send_sems.at[1],
            recv_sem=recv_sems.at[1],
            device_id=(lev * own_rows + row, target),
            device_id_type=MESH,
        )

    def start_b(k, carry):
        row, target, here = place_b(k)

        @pl.when(here)
        def _():
            pltpu.make_async_copy(send_b.at[target, row], recv_b.at[wave], recv_sems.at[1]).start()

        @pl.when(jnp.logical_not(here))
        def _():
            copy_b(row, target).start()

        return carry

    lax.fori_loop(0, waves, start_b, 0)
    pltpu.make_async_copy(recv_b, recv_b, recv_sems.at[1]).wait()

    received = recv_b[...].astype(F32).reshape(total_rows, LANES)
    for block in range(total_rows // LANES):
        flipped = received[block * LANES : (block + 1) * LANES, :].T
        for third in range(THIRDS):
            at_lane = third * total_rows + block * LANES
            channels[:, at_lane : at_lane + LANES] = flipped[
                third * PITCH : (third + 1) * PITCH, :
            ].astype(BF16)
    chunk = 3 * LANES if points % (3 * LANES) == 0 else LANES
    for first in range(0, points, chunk):
        inside = first + lax.broadcasted_iota(jnp.int32, (CHANNELS, chunk), 1) < length
        grid = jnp.dot(
            channels[0:CHANNELS, :], phase[:, first : first + chunk], preferred_element_type=F32
        )
        grid = jnp.where(inside, grid, F32(0.0)).astype(BF16)
        grid_out[:, first : first + chunk] = grid
        both = grid.astype(F32) + forcing[:, first : first + chunk].astype(F32)
        summed[:, first : first + chunk] = jnp.where(inside, both, F32(0.0)).astype(BF16)
    scale = quadrature[0] / length_f
    plane[...] = jnp.zeros_like(plane)
    for block in range(total_rows // LANES):
        for third in range(THIRDS):
            first = third * total_rows + block * LANES
            back = lax.dot_general(
                summed[...], phase[first : first + LANES, :], NT_DIMS, preferred_element_type=F32
            )
            plane[third * PITCH : third * PITCH + CHANNELS, :] = back * scale
        send_c[block * LANES // ROWS : (block + 1) * LANES // ROWS] = (
            plane[...].T.astype(BF16).reshape(LANES // ROWS, ROWS, LANES)
        )

    def copy_c(k):
        target = lax.rem(wave + k, waves)
        return pltpu.make_async_remote_copy(
            src_ref=send_c.at[target],
            dst_ref=recv_c.at[wave],
            send_sem=send_sems.at[2],
            recv_sem=recv_sems.at[2],
            device_id=(target, lev),
            device_id_type=MESH,
        )

    def start_c(k, carry):
        copy_c(k).start()
        return carry

    lax.fori_loop(1, waves, start_c, 0)
    pltpu.make_async_copy(send_c.at[wave], recv_c.at[wave], recv_sems.at[2]).start()
    pltpu.make_async_copy(recv_c, recv_c, recv_sems.at[2]).wait()

    spread[0:total_rows, :] = recv_c[...].astype(F32).reshape(total_rows, LANES)
    for row in range(ROWS):
        turned[row * LANES : (row + 1) * LANES, 0:waves] = spread[
            pl.ds(row, waves, stride=ROWS), :
        ].T
    for s, third, group in slots_of():
        for part_at in range(2):
            base = (group * 2 + part_at) * LANES + third * PITCH
            north = turned[pl.ds(base, PITCH // 2, stride=2), :]
            south = turned[pl.ds(base + 1, PITCH // 2, stride=2), :]
            joined = jnp.concatenate([north[:, 0:waves], south[:, 0:waves]], axis=1)
            plane[pl.ds(part_at, PITCH // 2, stride=2), 0 : 2 * waves] = joined
        spectra_out[s] = jnp.dot(
            plane[0:CHANNELS, 0 : 2 * waves].astype(BF16), weights[s], preferred_element_type=F32
        ).astype(BF16)

    def sent_a(k, carry):
        copy_a(lax.rem(lev + k, levs)).wait_send()
        return carry

    lax.fori_loop(1, levs, sent_a, 0)

    def sent_b(k, carry):
        row, target, here = place_b(k)

        @pl.when(jnp.logical_not(here))
        def _():
            copy_b(row, target).wait_send()

        return carry

    lax.fori_loop(0, waves, sent_b, 0)

    def sent_c(k, carry):
        copy_c(k).wait_send()
        return carry

    lax.fori_loop(1, waves, sent_c, 0)


def body(waves, levs, spectra, vertical, legendre, tile_mask, assign, row_points, quadrature, forcing):
    slots, fields, levels, parts, degrees = spectra.shape
    points = forcing.shape[-1]
    own_rows = waves // levs
    part = own_rows * ROWS
    total_rows = waves * ROWS
    smem = pl.BlockSpec(memory_space=pltpu.SMEM)
    vmem = pl.BlockSpec(memory_space=pltpu.VMEM)
    turned_rows = max(levs, ROWS) * LANES
    grid, spectra_out = pl.pallas_call(
        functools.partial(kernel, waves, levs),
        out_shape=(
            jax.ShapeDtypeStruct((CHANNELS, points), BF16),
            jax.ShapeDtypeStruct((slots, CHANNELS, degrees), BF16),
        ),
        in_specs=[vmem, vmem, smem, smem, smem, smem, vmem, vmem],
        out_specs=(vmem, vmem),
        scratch_shapes=[
            pltpu.VMEM((slots, 2 * waves, degrees), BF16),
            pltpu.VMEM((levs * LEVEL_PITCH, levs * LEVEL_PITCH), BF16),
            pltpu.VMEM((THIRDS * total_rows, points), BF16),
            pltpu.VMEM((LANES, LANES), F32),
            pltpu.VMEM((levs * LANES + 8, LANES), F32),
            pltpu.VMEM((turned_rows, LANES), F32),
            pltpu.VMEM((total_rows + 8, LANES), F32),
            pltpu.VMEM((PITCH, THIRDS * total_rows), BF16),
            pltpu.VMEM((CHANNELS, points), BF16),
            pltpu.VMEM((total_rows, LANES), BF16),
            pltpu.VMEM((levs, part, LANES), BF16),
            pltpu.VMEM((levs, own_rows, ROWS, LANES), BF16),
            pltpu.VMEM((waves, ROWS, LANES), BF16),
            pltpu.VMEM((waves, ROWS, LANES), BF16),
            pltpu.VMEM((waves, ROWS, LANES), BF16),
            pltpu.SemaphoreType.DMA((3,)),
            pltpu.SemaphoreType.DMA((3,)),
        ],
        compiler_params=pltpu.CompilerParams(
            collective_id=0, has_side_effects=True, vmem_limit_bytes=56 * 1024 * 1024
        ),
    )(
        spectra.reshape(slots, CHANNELS, degrees),
        legendre,
        tile_mask.reshape(slots, tile_mask.shape[1]),
        assign,
        row_points,
        quadrature,
        vertical,
        forcing.reshape(CHANNELS, points),
    )
    return grid.reshape(forcing.shape), spectra_out.reshape(spectra.shape)


def solution(mesh):
    return jax.shard_map(
        functools.partial(body, mesh.shape["wave"], mesh.shape["lev"]),
        mesh=mesh,
        in_specs=(
            P("wave", None, "lev", None, None),
            P(),
            P("wave", None, None),
            P("wave", None, None),
            P(),
            P("wave"),
            P("wave"),
            P(None, "lev", None, "wave", None),
        ),
        out_specs=(P(None, "lev", None, "wave", None), P("wave", None, "lev", None, None)),
        check_vma=False,
    )
```

```python
import functools
import math

import jax
import jax.numpy as jnp
from jax import lax
from jax.experimental import pallas as pl
from jax.experimental.pallas import tpu as pltpu
from jax.sharding import PartitionSpec as P

MESH = pl.DeviceIdType.MESH
F32 = jnp.float32
BF16 = jnp.bfloat16
LANES = 128
FIELDS = 3
OWN_LEVELS = 6
SLOTS = 10
GROUPS = 4
THIRDS = 3
PITCH = 40
LEVEL_PITCH = 24
ROWS = 2 * GROUPS
CHANNELS = 2 * FIELDS * OWN_LEVELS
STEP_WAVES = 4
RING = 8
NT_DIMS = (((1,), (1,)), ((), ()))


def cosine_of_turns(turns):
    reduced = turns - jnp.round(turns)
    square = reduced * reduced
    terms = [(-1.0) ** k * (2.0 * math.pi) ** (2 * k) / math.factorial(2 * k) for k in range(9)]
    total = square * F32(terms[8]) + F32(terms[7])
    for term in terms[6::-1]:
        total = total * square + F32(term)
    return total


def turns_of(product, length, inverse):
    return (product - jnp.floor(product * inverse) * length) * inverse


def low(value, size):
    return value & (size - 1)


def high(value, size):
    return value >> (size.bit_length() - 1)


def far_first(index, size):
    step = (index + 1) >> 1
    return low(size // 2 + jnp.where((index & 1) == 0, step, -step), size)


def wave_partner(index, wave, waves):
    rows = waves // RING
    up = low(high(wave, RING) + far_first(high(index, RING), rows), rows)
    side = low(wave + far_first(low(index, RING), RING), RING)
    return up * RING + side


def lev_partner(index, lev, levs):
    chips = levs // 2
    chip = low((lev >> 1) + far_first(index >> 1, chips), chips)
    return chip * 2 + ((lev + index + 1) & 1)


def slots_of():
    return [(s, s // GROUPS, s % GROUPS) for s in range(SLOTS)]


def kernel(
    waves,
    levs,
    spectra,
    legendre,
    tiles,
    assign,
    row_points,
    quadrature,
    vertical,
    forcing,
    grid_out,
    spectra_out,
    weights,
    mixer,
    phase,
    plane,
    rows32,
    turned,
    spread,
    channels,
    summed,
    send_a,
    recv_a,
    send_b,
    recv_b,
    send_c,
    recv_c,
    spectra_in,
    legendre_in,
    forcing_in,
    grid_held,
    spectra_held,
    send_sems,
    recv_sems,
    load_sems,
    store_sems,
):
    wave = lax.axis_index("wave")
    lev = lax.axis_index("lev")
    own_rows = waves // levs
    part = own_rows * ROWS
    total_rows = waves * ROWS
    degrees = spectra.shape[3]
    points = forcing.shape[2]
    block_waves = LANES // ROWS
    blocks = waves // block_waves

    loads = []
    for at, (source, held) in enumerate(((legendre, legendre_in), (spectra, spectra_in))):
        load = pltpu.make_async_copy(source, held, load_sems.at[at])
        load.start()
        loads.append(load)
    load_forcing = pltpu.make_async_copy(forcing, forcing_in, load_sems.at[2])
    load_forcing.start()

    barrier = pltpu.get_barrier_semaphore()

    def greet_wave(k, carry):
        pl.semaphore_signal(
            barrier, inc=1, device_id=(wave_partner(k, wave, waves), lev), device_id_type=MESH
        )
        return carry

    def greet_lev(k, carry):
        pl.semaphore_signal(
            barrier, inc=1, device_id=(wave, lev_partner(k, lev, levs)), device_id_type=MESH
        )
        return carry

    lax.fori_loop(0, waves - 1, greet_wave, 0)
    lax.fori_loop(0, levs - 1, greet_lev, 0)

    turned[...] = jnp.zeros_like(turned)
    plane[...] = jnp.zeros_like(plane)
    degree = lax.broadcasted_iota(jnp.int32, (1, degrees), 1)
    lane = lax.broadcasted_iota(jnp.int32, (1, LANES), 1)
    half = degrees // (2 * LANES // 2)
    for load in loads:
        load.wait()
    for s, third, group in slots_of():
        wave_number = assign[wave * SLOTS + s]
        marks = jnp.concatenate(
            [
                jnp.where(lane < LANES // 2, tiles[s, 0, 2 * k], tiles[s, 0, 2 * k + 1])
                for k in range(half)
            ],
            axis=1,
        )
        offset = degree - wave_number
        live = jnp.where((marks > 0) & (offset >= 0), F32(1.0), F32(0.0))
        signed = jnp.where((offset & 1) == 0, live, -live)
        table = legendre_in[s].astype(F32)
        lath = table.shape[0]
        weights[s, 0:lath, :] = (table * live).astype(BF16)
        weights[s, lath : 2 * lath, :] = (table * signed).astype(BF16)
        factor = jnp.where(wave_number == 0, F32(1.0), F32(2.0))
        plane[0:CHANNELS, 0 : 2 * lath] = factor * lax.dot_general(
            spectra_in[s].reshape(CHANNELS, degrees), weights[s], NT_DIMS, preferred_element_type=F32
        )
        for part_at in range(2):
            block = plane[pl.ds(part_at, PITCH // 2, stride=2), :]
            row = group * 2 + part_at
            base = row * LANES + third * PITCH
            turned[pl.ds(base, PITCH // 2, stride=2), :] = block
            turned[pl.ds(base + 1, PITCH // 2, stride=2), :] = pltpu.roll(
                block, LANES - lath, axis=1
            )
    for row in range(ROWS):
        flipped = turned[row * LANES : (row + 1) * LANES, :].T
        spread[pl.ds(row, waves, stride=ROWS), :] = flipped[0:waves, :]
    send_a[...] = spread[0:total_rows, :].astype(BF16)

    pl.semaphore_wait(barrier, levs - 1 + waves - 1)

    def copy_a(target):
        return pltpu.make_async_remote_copy(
            src_ref=send_a.at[pl.ds(pl.multiple_of(target * part, part), part), :],
            dst_ref=recv_a.at[lev],
            send_sem=send_sems.at[0],
            recv_sem=recv_sems.at[0],
            device_id=(wave, target),
            device_id_type=MESH,
        )

    def start_a(k, carry):
        copy_a(lev_partner(k, lev, levs)).start()
        return carry

    lax.fori_loop(0, levs - 1, start_a, 0)
    own_a = pltpu.make_async_copy(
        send_a.at[pl.ds(pl.multiple_of(lev * part, part), part), :],
        recv_a.at[lev],
        recv_sems.at[0],
    )
    own_a.start()

    levels = vertical.shape[1]
    edge = levs * LEVEL_PITCH
    at_row = lax.broadcasted_iota(jnp.int32, (edge, levels), 0)
    at_level = lax.broadcasted_iota(jnp.int32, (edge, levels), 1)
    at_group = (at_row * 2731) >> 16
    at_inner = at_row - at_group * LEVEL_PITCH
    at_field = (at_inner * 43) >> 8
    wanted = at_group * OWN_LEVELS + at_inner - at_field * OWN_LEVELS
    mixed = jnp.zeros((edge, edge), F32)
    for field in range(FIELDS):
        pick = jnp.where((at_field == field) & (at_level == wanted), F32(1.0), F32(0.0)).astype(
            BF16
        )
        rows = jnp.dot(pick, vertical[field], preferred_element_type=F32).astype(BF16)
        mixed = mixed + lax.dot_general(rows, pick, NT_DIMS, preferred_element_type=F32)
    mixer[...] = mixed.astype(BF16)

    length = row_points[0]
    length_f = length.astype(F32)
    inverse = F32(1.0) / length_f
    tall = STEP_WAVES * ROWS
    at = lax.broadcasted_iota(jnp.int32, (tall, LANES), 0)
    at_pair = at >> 1
    odd = jnp.concatenate([(at & 1) == 1] * THIRDS, axis=0)
    quarters = jnp.where(odd, F32(0.25), F32(0.0))
    column = lax.broadcasted_iota(jnp.int32, (THIRDS * tall, LANES), 1).astype(F32)
    group_at = at_pair & (GROUPS - 1)
    real = jnp.concatenate(
        [jnp.where(group_at < SLOTS - third * GROUPS, F32(1.0), F32(0.0)) for third in range(THIRDS)],
        axis=0,
    )
    steps = waves // STEP_WAVES

    def phase_rows(step, carry):
        numbers = []
        for third in range(THIRDS):
            number = jnp.zeros((tall, LANES), jnp.int32)
            for near in range(STEP_WAVES):
                for group in range(GROUPS):
                    s = third * GROUPS + group
                    if s < SLOTS:
                        held = assign[(step * STEP_WAVES + near) * SLOTS + s]
                        number = jnp.where(at_pair == near * GROUPS + group, held, number)
            numbers.append(number)
        number = jnp.concatenate(numbers, axis=0)
        kept = jnp.where(2 * number < length, real, F32(0.0))
        number = number.astype(F32)
        before = kept * cosine_of_turns(turns_of(number * column, length_f, inverse) + quarters)
        now = kept * cosine_of_turns(
            turns_of(number * (column + F32(LANES)), length_f, inverse) + quarters
        )
        first = jnp.broadcast_to(now[:, 0:1], now.shape)
        twice = F32(2.0) * jnp.where(odd, pltpu.roll(first, 1, axis=0), first)
        for block in range(points // LANES):
            value = before.astype(BF16)
            for third in range(THIRDS):
                phase[
                    pl.ds(pl.multiple_of(third * total_rows + step * tall, tall), tall),
                    block * LANES : (block + 1) * LANES,
                ] = value[third * tall : (third + 1) * tall, :]
            before, now = now, twice * now - before
        return carry

    lax.fori_loop(0, steps * 3 // 8, phase_rows, 0)

    whole_a = pltpu.make_async_copy(recv_a, recv_a, recv_sems.at[0])
    whole_a.wait()
    for source in range(levs):
        rows32[source * LANES : (source + 1) * LANES, 0:part] = recv_a[source].astype(F32).T
    for third in range(THIRDS):
        for side in range(2):
            start = third * PITCH + side
            block = jnp.concatenate(
                [
                    rows32[pl.ds(source * LANES + start, LEVEL_PITCH, stride=2), :]
                    for source in range(levs)
                ],
                axis=0,
            ).astype(BF16)
            product = jnp.dot(mixer[...], block, preferred_element_type=F32)
            for target in range(levs):
                turned[pl.ds(target * LANES + start, PITCH // 2, stride=2), :] = product[
                    target * LEVEL_PITCH : target * LEVEL_PITCH + PITCH // 2, :
                ]
    for target in range(levs):
        flipped = turned[target * LANES : (target + 1) * LANES, :].T[0:part, :]
        send_b[target] = flipped.astype(BF16).reshape(own_rows, ROWS, LANES)

    def place_b(k):
        target = lev_partner(high(k, own_rows), lev, levs)
        row = low(k, own_rows)
        return row, target, (lev * own_rows + row == wave) & (target == lev)

    def copy_b(row, target):
        return pltpu.make_async_remote_copy(
            src_ref=send_b.at[target, row],
            dst_ref=recv_b.at[wave],
            send_sem=send_sems.at[1],
            recv_sem=recv_sems.at[1],
            device_id=(lev * own_rows + row, target),
            device_id_type=MESH,
        )

    def start_b(k, carry):
        row, target, here = place_b(k)

        @pl.when(here)
        def _():
            pltpu.make_async_copy(
                send_b.at[target, row], recv_b.at[wave], recv_sems.at[1]
            ).start()

        @pl.when(jnp.logical_not(here))
        def _():
            copy_b(row, target).start()

        return carry

    lax.fori_loop(0, waves, start_b, 0)
    lax.fori_loop(steps * 3 // 8, steps, phase_rows, 0)

    load_forcing.wait()
    chunk = 3 * LANES if points % (3 * LANES) == 0 else LANES
    pltpu.make_async_copy(recv_b, recv_b, recv_sems.at[1]).wait()
    received = recv_b[...].astype(F32).reshape(total_rows, LANES)
    for block in range(blocks):
        flipped = received[block * LANES : (block + 1) * LANES, :].T
        for third in range(THIRDS):
            at_lane = third * total_rows + block * LANES
            channels[:, at_lane : at_lane + LANES] = flipped[
                third * PITCH : (third + 1) * PITCH, :
            ].astype(BF16)
    for first in range(0, points, chunk):
        inside = first + lax.broadcasted_iota(jnp.int32, (CHANNELS, chunk), 1) < length
        grid = jnp.dot(
            channels[0:CHANNELS, :], phase[:, first : first + chunk], preferred_element_type=F32
        )
        grid = jnp.where(inside, grid, F32(0.0)).astype(BF16)
        grid_held[:, :, first : first + chunk] = grid.reshape(CHANNELS // 2, 2, chunk)
        added = forcing_in[:, :, first : first + chunk].reshape(CHANNELS, chunk).astype(F32)
        both = jnp.where(inside, grid.astype(F32) + added, F32(0.0))
        summed[:, first : first + chunk] = both.astype(BF16)
    store_grid = pltpu.make_async_copy(grid_held, grid_out, store_sems.at[0])
    store_grid.start()
    scale = quadrature[0] / length_f
    plane[...] = jnp.zeros_like(plane)

    def copy_c(target):
        return pltpu.make_async_remote_copy(
            src_ref=send_c.at[target],
            dst_ref=recv_c.at[wave],
            send_sem=send_sems.at[2],
            recv_sem=recv_sems.at[2],
            device_id=(target, lev),
            device_id_type=MESH,
        )

    for block in range(blocks):
        for third in range(THIRDS):
            first = third * total_rows + block * LANES
            back = lax.dot_general(
                summed[...], phase[first : first + LANES, :], NT_DIMS, preferred_element_type=F32
            )
            plane[third * PITCH : third * PITCH + CHANNELS, :] = back * scale
        send_c[block * block_waves : (block + 1) * block_waves] = (
            plane[...].T.astype(BF16).reshape(block_waves, ROWS, LANES)
        )

    def start_c(k, carry):
        copy_c(wave_partner(k, wave, waves)).start()
        return carry

    lax.fori_loop(0, waves - 1, start_c, 0)
    pltpu.make_async_copy(send_c.at[wave], recv_c.at[wave], recv_sems.at[2]).start()
    pltpu.make_async_copy(recv_c, recv_c, recv_sems.at[2]).wait()

    spread[0:total_rows, :] = recv_c[...].astype(F32).reshape(total_rows, LANES)
    for row in range(ROWS):
        turned[row * LANES : (row + 1) * LANES, 0:waves] = spread[
            pl.ds(row, waves, stride=ROWS), :
        ].T
    for s, third, group in slots_of():
        for part_at in range(2):
            base = (group * 2 + part_at) * LANES + third * PITCH
            north = turned[pl.ds(base, PITCH // 2, stride=2), :]
            south = turned[pl.ds(base + 1, PITCH // 2, stride=2), :]
            joined = jnp.concatenate([north[:, 0:waves], south[:, 0:waves]], axis=1)
            plane[pl.ds(part_at, PITCH // 2, stride=2), 0 : 2 * waves] = joined
        spectra_held[s] = jnp.dot(
            plane[0:CHANNELS, 0 : 2 * waves].astype(BF16), weights[s], preferred_element_type=F32
        ).astype(BF16).reshape(CHANNELS // 2, 2, degrees)
    store_spectra = pltpu.make_async_copy(spectra_held, spectra_out, store_sems.at[1])
    store_spectra.start()

    def sent_a(k, carry):
        copy_a(lev_partner(k, lev, levs)).wait_send()
        return carry

    lax.fori_loop(0, levs - 1, sent_a, 0)

    def sent_b(k, carry):
        row, target, here = place_b(k)

        @pl.when(jnp.logical_not(here))
        def _():
            copy_b(row, target).wait_send()

        return carry

    lax.fori_loop(0, waves, sent_b, 0)

    def sent_c(k, carry):
        copy_c(low(wave + k, waves)).wait_send()
        return carry

    lax.fori_loop(1, waves, sent_c, 0)
    store_spectra.wait()
    store_grid.wait()


def body(waves, levs, spectra, vertical, legendre, tile_mask, assign, row_points, quadrature, forcing):
    slots, fields, levels, parts, degrees = spectra.shape
    points = forcing.shape[-1]
    own_rows = waves // levs
    part = own_rows * ROWS
    total_rows = waves * ROWS
    smem = pl.BlockSpec(memory_space=pltpu.SMEM)
    vmem = pl.BlockSpec(memory_space=pltpu.VMEM)
    hbm = pl.BlockSpec(memory_space=pl.ANY)
    turned_rows = max(levs, ROWS) * LANES
    grid, spectra_out = pl.pallas_call(
        functools.partial(kernel, waves, levs),
        out_shape=(
            jax.ShapeDtypeStruct((CHANNELS // 2, 2, points), BF16),
            jax.ShapeDtypeStruct((slots, CHANNELS // 2, 2, degrees), BF16),
        ),
        in_specs=[hbm, hbm, smem, smem, smem, smem, vmem, hbm],
        out_specs=(hbm, hbm),
        scratch_shapes=[
            pltpu.VMEM((slots, 2 * waves, degrees), BF16),
            pltpu.VMEM((levs * LEVEL_PITCH, levs * LEVEL_PITCH), BF16),
            pltpu.VMEM((THIRDS * total_rows, points), BF16),
            pltpu.VMEM((LANES, LANES), F32),
            pltpu.VMEM((levs * LANES + 8, LANES), F32),
            pltpu.VMEM((turned_rows, LANES), F32),
            pltpu.VMEM((total_rows + 8, LANES), F32),
            pltpu.VMEM((PITCH, THIRDS * total_rows), BF16),
            pltpu.VMEM((CHANNELS, points), BF16),
            pltpu.VMEM((total_rows, LANES), BF16),
            pltpu.VMEM((levs, part, LANES), BF16),
            pltpu.VMEM((levs, own_rows, ROWS, LANES), BF16),
            pltpu.VMEM((waves, ROWS, LANES), BF16),
            pltpu.VMEM((waves, ROWS, LANES), BF16),
            pltpu.VMEM((waves, ROWS, LANES), BF16),
            pltpu.VMEM((slots, CHANNELS // 2, 2, degrees), BF16),
            pltpu.VMEM(legendre.shape, BF16),
            pltpu.VMEM((CHANNELS // 2, 2, points), BF16),
            pltpu.VMEM((CHANNELS // 2, 2, points), BF16),
            pltpu.VMEM((slots, CHANNELS // 2, 2, degrees), BF16),
            pltpu.SemaphoreType.DMA((3,)),
            pltpu.SemaphoreType.DMA((3,)),
            pltpu.SemaphoreType.DMA((3,)),
            pltpu.SemaphoreType.DMA((2,)),
        ],
        compiler_params=pltpu.CompilerParams(
            collective_id=0, has_side_effects=True, vmem_limit_bytes=56 * 1024 * 1024
        ),
    )(
        spectra.reshape(slots, CHANNELS // 2, 2, degrees),
        legendre,
        jnp.transpose(tile_mask, (0, 2, 1)),
        assign,
        row_points,
        quadrature,
        vertical,
        forcing.reshape(CHANNELS // 2, 2, points),
    )
    return grid.reshape(forcing.shape), spectra_out.reshape(spectra.shape)


def solution(mesh):
    return jax.shard_map(
        functools.partial(body, mesh.shape["wave"], mesh.shape["lev"]),
        mesh=mesh,
        in_specs=(
            P("wave", None, "lev", None, None),
            P(),
            P("wave", None, None),
            P("wave", None, None),
            P(),
            P("wave"),
            P("wave"),
            P(None, "lev", None, "wave", None),
        ),
        out_specs=(P(None, "lev", None, "wave", None), P("wave", None, "lev", None, None)),
        check_vma=False,
    )
```

```python
import functools
import math

import jax
import jax.numpy as jnp
from jax import lax
from jax.experimental import pallas as pl
from jax.experimental.pallas import tpu as pltpu
from jax.sharding import PartitionSpec as P

MESH = pl.DeviceIdType.MESH
F32 = jnp.float32
BF16 = jnp.bfloat16
LANES = 128
FIELDS = 3
OWN_LEVELS = 6
SLOTS = 10
GROUPS = 4
THIRDS = 3
PITCH = 40
LEVEL_PITCH = 24
ROWS = 2 * GROUPS
CHANNELS = 2 * FIELDS * OWN_LEVELS
STEP_WAVES = 4
VMEM_BYTES = 56 * 1024 * 1024
RING = 8
NT_DIMS = (((1,), (1,)), ((), ()))


def cosine_of_turns(turns):
    reduced = turns - jnp.round(turns)
    square = reduced * reduced
    terms = [(-1.0) ** k * (2.0 * math.pi) ** (2 * k) / math.factorial(2 * k) for k in range(9)]
    total = square * F32(terms[8]) + F32(terms[7])
    for term in terms[6::-1]:
        total = total * square + F32(term)
    return total


def turns_of(product, length, inverse):
    return (product - jnp.floor(product * inverse) * length) * inverse


def low(value, size):
    return value & (size - 1)


def high(value, size):
    return value >> (size.bit_length() - 1)


def far_first(index, size):
    step = (index + 1) >> 1
    return low(size // 2 + jnp.where((index & 1) == 0, step, -step), size)


def wave_partner(index, wave, waves):
    rows = waves // RING
    up = low(high(wave, RING) + far_first(high(index, RING), rows), rows)
    side = low(wave + far_first(low(index, RING), RING), RING)
    return up * RING + side


def lev_partner(index, lev, levs):
    chips = levs // 2
    chip = low((lev >> 1) + far_first(index >> 1, chips), chips)
    return chip * 2 + ((lev + index + 1) & 1)


def slots_of():
    return [(s, s // GROUPS, s % GROUPS) for s in range(SLOTS)]


def kernel(
    waves,
    levs,
    spectra,
    legendre,
    tiles,
    assign,
    row_points,
    quadrature,
    vertical,
    forcing,
    grid_out,
    spectra_out,
    weights,
    mixer,
    phase,
    plane,
    rows32,
    turned,
    spread,
    channels,
    summed,
    send_a,
    recv_a,
    send_b,
    recv_b,
    send_c,
    recv_c,
    spectra_in,
    legendre_in,
    forcing_in,
    vertical_in,
    tiles_in,
    assign_in,
    row_points_in,
    quadrature_in,
    grid_held,
    spectra_held,
    send_sems,
    recv_sems,
    load_sems,
    store_sems,
):
    wave = lax.axis_index("wave")
    lev = lax.axis_index("lev")
    own_rows = waves // levs
    part = own_rows * ROWS
    total_rows = waves * ROWS
    degrees = spectra.shape[3]
    points = forcing.shape[2]
    block_waves = LANES // ROWS
    blocks = waves // block_waves

    pairs = (
        (assign, assign_in),
        (tiles, tiles_in),
        (legendre, legendre_in),
        (spectra, spectra_in),
        (vertical, vertical_in),
        (row_points, row_points_in),
        (quadrature, quadrature_in),
        (forcing, forcing_in),
    )
    loads = [
        pltpu.make_async_copy(source, held, load_sems.at[at])
        for at, (source, held) in enumerate(pairs)
    ]
    for load in loads:
        load.start()

    barrier = pltpu.get_barrier_semaphore()

    def greet_wave(k, carry):
        pl.semaphore_signal(
            barrier, inc=1, device_id=(wave_partner(k, wave, waves), lev), device_id_type=MESH
        )
        return carry

    def greet_lev(k, carry):
        pl.semaphore_signal(
            barrier, inc=1, device_id=(wave, lev_partner(k, lev, levs)), device_id_type=MESH
        )
        return carry

    lax.fori_loop(0, waves - 1, greet_wave, 0)
    lax.fori_loop(0, levs - 1, greet_lev, 0)

    turned[...] = jnp.zeros_like(turned)
    plane[...] = jnp.zeros_like(plane)
    degree = lax.broadcasted_iota(jnp.int32, (1, degrees), 1)
    lane = lax.broadcasted_iota(jnp.int32, (1, LANES), 1)
    half = degrees // (2 * LANES // 2)
    for load in loads:
        load.wait()
    for s, third, group in slots_of():
        wave_number = assign_in[wave * SLOTS + s]
        marks = jnp.concatenate(
            [
                jnp.where(lane < LANES // 2, tiles_in[s, 0, 2 * k], tiles_in[s, 0, 2 * k + 1])
                for k in range(half)
            ],
            axis=1,
        )
        offset = degree - wave_number
        live = jnp.where((marks > 0) & (offset >= 0), F32(1.0), F32(0.0))
        signed = jnp.where((offset & 1) == 0, live, -live)
        table = legendre_in[s].astype(F32)
        lath = table.shape[0]
        weights[s, 0:lath, :] = (table * live).astype(BF16)
        weights[s, lath : 2 * lath, :] = (table * signed).astype(BF16)
        factor = jnp.where(wave_number == 0, F32(1.0), F32(2.0))
        plane[0:CHANNELS, 0 : 2 * lath] = factor * lax.dot_general(
            spectra_in[s].reshape(CHANNELS, degrees), weights[s], NT_DIMS, preferred_element_type=F32
        )
        for part_at in range(2):
            block = plane[pl.ds(part_at, PITCH // 2, stride=2), :]
            row = group * 2 + part_at
            base = row * LANES + third * PITCH
            turned[pl.ds(base, PITCH // 2, stride=2), :] = block
            turned[pl.ds(base + 1, PITCH // 2, stride=2), :] = pltpu.roll(
                block, LANES - lath, axis=1
            )
    for row in range(ROWS):
        flipped = turned[row * LANES : (row + 1) * LANES, :].T
        spread[pl.ds(row, waves, stride=ROWS), :] = flipped[0:waves, :]
    send_a[...] = spread[0:total_rows, :].astype(BF16)

    levels = vertical_in.shape[1]
    edge = levs * LEVEL_PITCH
    at_row = lax.broadcasted_iota(jnp.int32, (edge, levels), 0)
    at_level = lax.broadcasted_iota(jnp.int32, (edge, levels), 1)
    at_group = (at_row * 2731) >> 16
    at_inner = at_row - at_group * LEVEL_PITCH
    at_field = (at_inner * 43) >> 8
    wanted = at_group * OWN_LEVELS + at_inner - at_field * OWN_LEVELS
    mixed = jnp.zeros((edge, edge), F32)
    for field in range(FIELDS):
        pick = jnp.where((at_field == field) & (at_level == wanted), F32(1.0), F32(0.0)).astype(
            BF16
        )
        rows = jnp.dot(pick, vertical_in[field], preferred_element_type=F32).astype(BF16)
        mixed = mixed + lax.dot_general(rows, pick, NT_DIMS, preferred_element_type=F32)
    mixer[...] = mixed.astype(BF16)

    pl.semaphore_wait(barrier, levs - 1 + waves - 1)

    def copy_a(target):
        return pltpu.make_async_remote_copy(
            src_ref=send_a.at[pl.ds(pl.multiple_of(target * part, part), part), :],
            dst_ref=recv_a.at[lev],
            send_sem=send_sems.at[0],
            recv_sem=recv_sems.at[0],
            device_id=(wave, target),
            device_id_type=MESH,
        )

    def start_a(k, carry):
        copy_a(lev_partner(k, lev, levs)).start()
        return carry

    lax.fori_loop(0, levs - 1, start_a, 0)
    own_a = pltpu.make_async_copy(
        send_a.at[pl.ds(pl.multiple_of(lev * part, part), part), :],
        recv_a.at[lev],
        recv_sems.at[0],
    )
    own_a.start()

    length = row_points_in[0]
    length_f = length.astype(F32)
    inverse = F32(1.0) / length_f
    tall = STEP_WAVES * ROWS
    at = lax.broadcasted_iota(jnp.int32, (tall, LANES), 0)
    at_pair = at >> 1
    odd = jnp.concatenate([(at & 1) == 1] * THIRDS, axis=0)
    quarters = jnp.where(odd, F32(0.25), F32(0.0))
    column = lax.broadcasted_iota(jnp.int32, (THIRDS * tall, LANES), 1).astype(F32)
    group_at = at_pair & (GROUPS - 1)
    real = jnp.concatenate(
        [jnp.where(group_at < SLOTS - third * GROUPS, F32(1.0), F32(0.0)) for third in range(THIRDS)],
        axis=0,
    )
    steps = waves // STEP_WAVES

    def phase_rows(step, carry):
        numbers = []
        for third in range(THIRDS):
            number = jnp.zeros((tall, LANES), jnp.int32)
            for near in range(STEP_WAVES):
                for group in range(GROUPS):
                    s = third * GROUPS + group
                    if s < SLOTS:
                        held = assign_in[(step * STEP_WAVES + near) * SLOTS + s]
                        number = jnp.where(at_pair == near * GROUPS + group, held, number)
            numbers.append(number)
        number = jnp.concatenate(numbers, axis=0)
        kept = jnp.where(2 * number < length, real, F32(0.0))
        number = number.astype(F32)
        before = kept * cosine_of_turns(turns_of(number * column, length_f, inverse) + quarters)
        now = kept * cosine_of_turns(
            turns_of(number * (column + F32(LANES)), length_f, inverse) + quarters
        )
        first = jnp.broadcast_to(now[:, 0:1], now.shape)
        twice = F32(2.0) * jnp.where(odd, pltpu.roll(first, 1, axis=0), first)
        for block in range(points // LANES):
            value = before.astype(BF16)
            for third in range(THIRDS):
                phase[
                    pl.ds(pl.multiple_of(third * total_rows + step * tall, tall), tall),
                    block * LANES : (block + 1) * LANES,
                ] = value[third * tall : (third + 1) * tall, :]
            before, now = now, twice * now - before
        return carry

    lax.fori_loop(0, steps * 3 // 8, phase_rows, 0)

    whole_a = pltpu.make_async_copy(recv_a, recv_a, recv_sems.at[0])
    whole_a.wait()
    for source in range(levs):
        rows32[source * LANES : (source + 1) * LANES, 0:part] = recv_a[source].astype(F32).T
    for third in range(THIRDS):
        for side in range(2):
            start = third * PITCH + side
            block = jnp.concatenate(
                [
                    rows32[pl.ds(source * LANES + start, LEVEL_PITCH, stride=2), :]
                    for source in range(levs)
                ],
                axis=0,
            ).astype(BF16)
            product = jnp.dot(mixer[...], block, preferred_element_type=F32)
            for target in range(levs):
                turned[pl.ds(target * LANES + start, PITCH // 2, stride=2), :] = product[
                    target * LEVEL_PITCH : target * LEVEL_PITCH + PITCH // 2, :
                ]
    for target in range(levs):
        flipped = turned[target * LANES : (target + 1) * LANES, :].T[0:part, :]
        send_b[target] = flipped.astype(BF16).reshape(own_rows, ROWS, LANES)

    def place_b(k):
        target = lev_partner(high(k, own_rows), lev, levs)
        row = low(k, own_rows)
        return row, target, (lev * own_rows + row == wave) & (target == lev)

    def copy_b(row, target):
        return pltpu.make_async_remote_copy(
            src_ref=send_b.at[target, row],
            dst_ref=recv_b.at[wave],
            send_sem=send_sems.at[1],
            recv_sem=recv_sems.at[1],
            device_id=(lev * own_rows + row, target),
            device_id_type=MESH,
        )

    def start_b(k, carry):
        row, target, here = place_b(k)

        @pl.when(here)
        def _():
            pltpu.make_async_copy(
                send_b.at[target, row], recv_b.at[wave], recv_sems.at[1]
            ).start()

        @pl.when(jnp.logical_not(here))
        def _():
            copy_b(row, target).start()

        return carry

    lax.fori_loop(0, waves, start_b, 0)
    lax.fori_loop(steps * 3 // 8, steps, phase_rows, 0)

    chunk = 3 * LANES if points % (3 * LANES) == 0 else LANES
    pltpu.make_async_copy(recv_b, recv_b, recv_sems.at[1]).wait()
    received = recv_b[...].astype(F32).reshape(total_rows, LANES)
    for block in range(blocks):
        flipped = received[block * LANES : (block + 1) * LANES, :].T
        for third in range(THIRDS):
            at_lane = third * total_rows + block * LANES
            channels[:, at_lane : at_lane + LANES] = flipped[
                third * PITCH : (third + 1) * PITCH, :
            ].astype(BF16)
    for first in range(0, points, chunk):
        inside = first + lax.broadcasted_iota(jnp.int32, (CHANNELS, chunk), 1) < length
        grid = jnp.dot(
            channels[0:CHANNELS, :], phase[:, first : first + chunk], preferred_element_type=F32
        )
        grid = jnp.where(inside, grid, F32(0.0)).astype(BF16)
        grid_held[:, :, first : first + chunk] = grid.reshape(CHANNELS // 2, 2, chunk)
        added = forcing_in[:, :, first : first + chunk].reshape(CHANNELS, chunk).astype(F32)
        both = jnp.where(inside, grid.astype(F32) + added, F32(0.0))
        summed[:, first : first + chunk] = both.astype(BF16)
    store_grid = pltpu.make_async_copy(grid_held, grid_out, store_sems.at[0])
    store_grid.start()
    scale = quadrature_in[0] / length_f
    plane[...] = jnp.zeros_like(plane)

    def copy_c(target):
        return pltpu.make_async_remote_copy(
            src_ref=send_c.at[target],
            dst_ref=recv_c.at[wave],
            send_sem=send_sems.at[2],
            recv_sem=recv_sems.at[2],
            device_id=(target, lev),
            device_id_type=MESH,
        )

    for block in range(blocks):
        for third in range(THIRDS):
            first = third * total_rows + block * LANES
            back = lax.dot_general(
                summed[...], phase[first : first + LANES, :], NT_DIMS, preferred_element_type=F32
            )
            plane[third * PITCH : third * PITCH + CHANNELS, :] = back * scale
        send_c[block * block_waves : (block + 1) * block_waves] = (
            plane[...].T.astype(BF16).reshape(block_waves, ROWS, LANES)
        )

    def start_c(k, carry):
        copy_c(wave_partner(k, wave, waves)).start()
        return carry

    lax.fori_loop(0, waves - 1, start_c, 0)
    pltpu.make_async_copy(send_c.at[wave], recv_c.at[wave], recv_sems.at[2]).start()
    sent_a = send_a.at[pl.ds(0, (levs - 1) * part), :]
    pltpu.make_async_copy(sent_a, sent_a, send_sems.at[0]).wait()
    own_among = high(wave, own_rows) == lev

    def wait_sent(held, count, sem):
        sent = held.at[pl.ds(0, count)]
        pltpu.make_async_copy(sent, sent, sem).wait()

    @pl.when(own_among)
    def _():
        wait_sent(recv_b, waves - 1, send_sems.at[1])

    @pl.when(jnp.logical_not(own_among))
    def _():
        wait_sent(recv_b, waves, send_sems.at[1])

    wait_sent(send_c, waves - 1, send_sems.at[2])
    pltpu.make_async_copy(recv_c, recv_c, recv_sems.at[2]).wait()

    spread[0:total_rows, :] = recv_c[...].astype(F32).reshape(total_rows, LANES)
    for row in range(ROWS):
        turned[row * LANES : (row + 1) * LANES, 0:waves] = spread[
            pl.ds(row, waves, stride=ROWS), :
        ].T
    for s, third, group in slots_of():
        for part_at in range(2):
            base = (group * 2 + part_at) * LANES + third * PITCH
            north = turned[pl.ds(base, PITCH // 2, stride=2), :]
            south = turned[pl.ds(base + 1, PITCH // 2, stride=2), :]
            joined = jnp.concatenate([north[:, 0:waves], south[:, 0:waves]], axis=1)
            plane[pl.ds(part_at, PITCH // 2, stride=2), 0 : 2 * waves] = joined
        spectra_held[s] = jnp.dot(
            plane[0:CHANNELS, 0 : 2 * waves].astype(BF16), weights[s], preferred_element_type=F32
        ).astype(BF16).reshape(CHANNELS // 2, 2, degrees)
    store_spectra = pltpu.make_async_copy(spectra_held, spectra_out, store_sems.at[1])
    store_spectra.start()

    store_spectra.wait()
    store_grid.wait()


def hand_out(grid, spectra, grid_out, spectra_out, grid_held, spectra_held, sems):
    loads = [
        pltpu.make_async_copy(spectra, spectra_held, sems.at[0]),
        pltpu.make_async_copy(grid, grid_held, sems.at[1]),
    ]
    stores = [
        pltpu.make_async_copy(spectra_held, spectra_out, sems.at[2]),
        pltpu.make_async_copy(grid_held, grid_out, sems.at[3]),
    ]
    for load in loads:
        load.start()
    for load, store in zip(loads, stores):
        load.wait()
        store.start()
    for store in stores:
        store.wait()


def body(waves, levs, spectra, vertical, legendre, tile_mask, assign, row_points, quadrature, forcing):
    slots, fields, levels, parts, degrees = spectra.shape
    points = forcing.shape[-1]
    own_rows = waves // levs
    part = own_rows * ROWS
    total_rows = waves * ROWS
    hbm = pl.BlockSpec(memory_space=pl.ANY)
    turned_rows = max(levs, ROWS) * LANES
    grid, spectra_out = pl.pallas_call(
        functools.partial(kernel, waves, levs),
        out_shape=(
            jax.ShapeDtypeStruct((CHANNELS // 2, 2, points), BF16),
            jax.ShapeDtypeStruct((slots, CHANNELS // 2, 2, degrees), BF16),
        ),
        in_specs=[hbm] * 8,
        out_specs=(hbm, hbm),
        scratch_shapes=[
            pltpu.VMEM((slots, 2 * waves, degrees), BF16),
            pltpu.VMEM((levs * LEVEL_PITCH, levs * LEVEL_PITCH), BF16),
            pltpu.VMEM((THIRDS * total_rows, points), BF16),
            pltpu.VMEM((LANES, LANES), F32),
            pltpu.VMEM((levs * LANES + 8, LANES), F32),
            pltpu.VMEM((turned_rows, LANES), F32),
            pltpu.VMEM((total_rows + 8, LANES), F32),
            pltpu.VMEM((PITCH, THIRDS * total_rows), BF16),
            pltpu.VMEM((CHANNELS, points), BF16),
            pltpu.VMEM((total_rows, LANES), BF16),
            pltpu.VMEM((levs, part, LANES), BF16),
            pltpu.VMEM((levs, own_rows, ROWS, LANES), BF16),
            pltpu.VMEM((waves, ROWS, LANES), BF16),
            pltpu.VMEM((waves, ROWS, LANES), BF16),
            pltpu.VMEM((waves, ROWS, LANES), BF16),
            pltpu.VMEM((slots, CHANNELS // 2, 2, degrees), BF16),
            pltpu.VMEM(legendre.shape, BF16),
            pltpu.VMEM((CHANNELS // 2, 2, points), BF16),
            pltpu.VMEM(vertical.shape, BF16),
            pltpu.SMEM((slots, 1, tile_mask.shape[1]), jnp.int32),
            pltpu.SMEM(assign.shape, jnp.int32),
            pltpu.SMEM(row_points.shape, jnp.int32),
            pltpu.SMEM(quadrature.shape, F32),
            pltpu.VMEM((CHANNELS // 2, 2, points), BF16),
            pltpu.VMEM((slots, CHANNELS // 2, 2, degrees), BF16),
            pltpu.SemaphoreType.DMA((3,)),
            pltpu.SemaphoreType.DMA((3,)),
            pltpu.SemaphoreType.DMA((8,)),
            pltpu.SemaphoreType.DMA((2,)),
        ],
        compiler_params=pltpu.CompilerParams(
            collective_id=0, has_side_effects=True, vmem_limit_bytes=VMEM_BYTES
        ),
    )(
        spectra.reshape(slots, CHANNELS // 2, 2, degrees),
        legendre,
        jnp.transpose(tile_mask, (0, 2, 1)),
        assign,
        row_points,
        quadrature,
        vertical,
        forcing.reshape(CHANNELS // 2, 2, points),
    )
    grid, spectra_out = pl.pallas_call(
        hand_out,
        out_shape=(
            jax.ShapeDtypeStruct(grid.shape, BF16),
            jax.ShapeDtypeStruct(spectra_out.shape, BF16),
        ),
        in_specs=[hbm, hbm],
        out_specs=(hbm, hbm),
        scratch_shapes=[
            pltpu.VMEM(grid.shape, BF16),
            pltpu.VMEM(spectra_out.shape, BF16),
            pltpu.SemaphoreType.DMA((4,)),
        ],
        compiler_params=pltpu.CompilerParams(vmem_limit_bytes=VMEM_BYTES),
    )(grid, spectra_out)
    return grid.reshape(forcing.shape), spectra_out.reshape(spectra.shape)


def solution(mesh):
    return jax.shard_map(
        functools.partial(body, mesh.shape["wave"], mesh.shape["lev"]),
        mesh=mesh,
        in_specs=(
            P("wave", None, "lev", None, None),
            P(),
            P("wave", None, None),
            P("wave", None, None),
            P(),
            P("wave"),
            P("wave"),
            P(None, "lev", None, "wave", None),
        ),
        out_specs=(P(None, "lev", None, "wave", None), P("wave", None, "lev", None, None)),
        check_vma=False,
    )
```

```python
import functools
import math

import jax
import jax.numpy as jnp
from jax import lax
from jax.experimental import pallas as pl
from jax.experimental.pallas import tpu as pltpu
from jax.sharding import PartitionSpec as P

MESH = pl.DeviceIdType.MESH
F32 = jnp.float32
BF16 = jnp.bfloat16
LANES = 128
FIELDS = 3
OWN_LEVELS = 6
SLOTS = 10
GROUPS = 4
THIRDS = 3
PITCH = 40
LEVEL_PITCH = 24
ROWS = 2 * GROUPS
CHANNELS = 2 * FIELDS * OWN_LEVELS
STEP_WAVES = 4
VMEM_BYTES = 56 * 1024 * 1024
RING = 8
NT_DIMS = (((1,), (1,)), ((), ()))


def cosine_of_turns(turns):
    reduced = turns - jnp.round(turns)
    square = reduced * reduced
    terms = [(-1.0) ** k * (2.0 * math.pi) ** (2 * k) / math.factorial(2 * k) for k in range(9)]
    total = square * F32(terms[8]) + F32(terms[7])
    for term in terms[6::-1]:
        total = total * square + F32(term)
    return total


def turns_of(product, length, inverse):
    return (product - jnp.floor(product * inverse) * length) * inverse


def low(value, size):
    return value & (size - 1)


def high(value, size):
    return value >> (size.bit_length() - 1)


def far_first(index, size):
    step = (index + 1) >> 1
    return low(size // 2 + jnp.where((index & 1) == 0, step, -step), size)


def wave_partner(index, wave, waves):
    rows = waves // RING
    up = low(high(wave, RING) + far_first(high(index, RING), rows), rows)
    side = low(wave + far_first(low(index, RING), RING), RING)
    return up * RING + side


def lev_partner(index, lev, levs):
    chips = levs // 2
    chip = low((lev >> 1) + far_first(index >> 1, chips), chips)
    return chip * 2 + ((lev + index + 1) & 1)


def slots_of():
    return [(s, s // GROUPS, s % GROUPS) for s in range(SLOTS)]


def kernel(
    waves,
    levs,
    spectra,
    legendre,
    tiles,
    assign,
    row_points,
    quadrature,
    vertical,
    forcing,
    grid_out,
    spectra_out,
    weights,
    mixer,
    phase,
    plane,
    rows32,
    turned,
    spread,
    channels,
    summed,
    send_a,
    recv_a,
    send_b,
    recv_b,
    send_c,
    recv_c,
    spectra_in,
    legendre_in,
    forcing_in,
    vertical_in,
    tiles_in,
    assign_in,
    row_points_in,
    quadrature_in,
    grid_held,
    spectra_held,
    send_sems,
    recv_sems,
    load_sems,
    store_sems,
    line_sem,
    plane_sem,
):
    wave = lax.axis_index("wave")
    lev = lax.axis_index("lev")
    own_rows = waves // levs
    part = own_rows * ROWS
    total_rows = waves * ROWS
    degrees = spectra.shape[3]
    points = forcing.shape[2]
    block_waves = LANES // ROWS
    blocks = waves // block_waves

    pairs = (
        (assign, assign_in),
        (tiles, tiles_in),
        (legendre, legendre_in),
        (spectra, spectra_in),
        (vertical, vertical_in),
        (row_points, row_points_in),
        (quadrature, quadrature_in),
        (forcing, forcing_in),
    )
    loads = [
        pltpu.make_async_copy(source, held, load_sems.at[at])
        for at, (source, held) in enumerate(pairs)
    ]
    for load in loads:
        load.start()

    barrier = pltpu.get_barrier_semaphore()

    core = lev & 1
    chip = lev >> 1
    chips = levs // 2

    def greet(row, column):
        pl.semaphore_signal(barrier, inc=1, device_id=(row, column), device_id_type=MESH)

    def greet_plane(k, carry):
        greet(wave_partner(k, wave, waves), chip * 2 + 1)
        return carry

    def greet_line(k, carry):
        greet(wave, low(chip + far_first(k, chips), chips) * 2)
        return carry

    lax.fori_loop(0, waves - 1, greet_plane, 0)
    lax.fori_loop(0, chips - 1, greet_line, 0)
    greet(wave, lev + 1 - 2 * core)

    turned[...] = jnp.zeros_like(turned)
    plane[...] = jnp.zeros_like(plane)
    degree = lax.broadcasted_iota(jnp.int32, (1, degrees), 1)
    lane = lax.broadcasted_iota(jnp.int32, (1, LANES), 1)
    half = degrees // (2 * LANES // 2)
    for load in loads:
        load.wait()
    for s, third, group in slots_of():
        wave_number = assign_in[wave * SLOTS + s]
        marks = jnp.concatenate(
            [
                jnp.where(lane < LANES // 2, tiles_in[s, 0, 2 * k], tiles_in[s, 0, 2 * k + 1])
                for k in range(half)
            ],
            axis=1,
        )
        offset = degree - wave_number
        live = jnp.where((marks > 0) & (offset >= 0), F32(1.0), F32(0.0))
        signed = jnp.where((offset & 1) == 0, live, -live)
        table = legendre_in[s].astype(F32)
        lath = table.shape[0]
        weights[s, 0:lath, :] = (table * live).astype(BF16)
        weights[s, lath : 2 * lath, :] = (table * signed).astype(BF16)
        factor = jnp.where(wave_number == 0, F32(1.0), F32(2.0))
        plane[0:CHANNELS, 0 : 2 * lath] = factor * lax.dot_general(
            spectra_in[s].reshape(CHANNELS, degrees), weights[s], NT_DIMS, preferred_element_type=F32
        )
        for part_at in range(2):
            block = plane[pl.ds(part_at, PITCH // 2, stride=2), :]
            row = group * 2 + part_at
            base = row * LANES + third * PITCH
            turned[pl.ds(base, PITCH // 2, stride=2), :] = block
            turned[pl.ds(base + 1, PITCH // 2, stride=2), :] = pltpu.roll(
                block, LANES - lath, axis=1
            )
    for row in range(ROWS):
        flipped = turned[row * LANES : (row + 1) * LANES, :].T
        spread[pl.ds(row, waves, stride=ROWS), :] = flipped[0:waves, :]
    send_a[...] = spread[0:total_rows, :].astype(BF16)

    levels = vertical_in.shape[1]
    edge = levs * LEVEL_PITCH
    at_row = lax.broadcasted_iota(jnp.int32, (edge, levels), 0)
    at_level = lax.broadcasted_iota(jnp.int32, (edge, levels), 1)
    at_group = (at_row * 2731) >> 16
    at_inner = at_row - at_group * LEVEL_PITCH
    at_field = (at_inner * 43) >> 8
    wanted = at_group * OWN_LEVELS + at_inner - at_field * OWN_LEVELS
    mixed = jnp.zeros((edge, edge), F32)
    for field in range(FIELDS):
        pick = jnp.where((at_field == field) & (at_level == wanted), F32(1.0), F32(0.0)).astype(
            BF16
        )
        rows = jnp.dot(pick, vertical_in[field], preferred_element_type=F32).astype(BF16)
        mixed = mixed + lax.dot_general(rows, pick, NT_DIMS, preferred_element_type=F32)
    mixer[...] = mixed.astype(BF16)

    @pl.when(core == 0)
    def _():
        pl.semaphore_wait(barrier, levs - 1)
        pl.semaphore_signal(line_sem, inc=1, device_id=(wave, lev + 1), device_id_type=MESH)

    @pl.when(core == 1)
    def _():
        pl.semaphore_wait(line_sem, 1)

    def copy_a(target):
        return pltpu.make_async_remote_copy(
            src_ref=send_a.at[pl.ds(pl.multiple_of(target * part, part), part), :],
            dst_ref=recv_a.at[lev],
            send_sem=send_sems.at[0],
            recv_sem=recv_sems.at[0],
            device_id=(wave, target),
            device_id_type=MESH,
        )

    def start_a(k, carry):
        copy_a(lev_partner(k, lev, levs)).start()
        return carry

    lax.fori_loop(0, levs - 1, start_a, 0)
    own_a = pltpu.make_async_copy(
        send_a.at[pl.ds(pl.multiple_of(lev * part, part), part), :],
        recv_a.at[lev],
        recv_sems.at[0],
    )
    own_a.start()

    @pl.when(core == 1)
    def _():
        pl.semaphore_wait(barrier, 2 * waves - 1)

        def tell(k, carry):
            pl.semaphore_signal(
                plane_sem,
                inc=1,
                device_id=(wave, lev_partner(k, lev, levs)),
                device_id_type=MESH,
            )
            return carry

        lax.fori_loop(0, levs - 1, tell, 0)

    length = row_points_in[0]
    length_f = length.astype(F32)
    inverse = F32(1.0) / length_f
    tall = STEP_WAVES * ROWS
    at = lax.broadcasted_iota(jnp.int32, (tall, LANES), 0)
    at_pair = at >> 1
    odd = jnp.concatenate([(at & 1) == 1] * THIRDS, axis=0)
    quarters = jnp.where(odd, F32(0.25), F32(0.0))
    column = lax.broadcasted_iota(jnp.int32, (THIRDS * tall, LANES), 1).astype(F32)
    group_at = at_pair & (GROUPS - 1)
    real = jnp.concatenate(
        [jnp.where(group_at < SLOTS - third * GROUPS, F32(1.0), F32(0.0)) for third in range(THIRDS)],
        axis=0,
    )
    steps = waves // STEP_WAVES

    def phase_rows(step, carry):
        numbers = []
        for third in range(THIRDS):
            number = jnp.zeros((tall, LANES), jnp.int32)
            for near in range(STEP_WAVES):
                for group in range(GROUPS):
                    s = third * GROUPS + group
                    if s < SLOTS:
                        held = assign_in[(step * STEP_WAVES + near) * SLOTS + s]
                        number = jnp.where(at_pair == near * GROUPS + group, held, number)
            numbers.append(number)
        number = jnp.concatenate(numbers, axis=0)
        kept = jnp.where(2 * number < length, real, F32(0.0))
        number = number.astype(F32)
        before = kept * cosine_of_turns(turns_of(number * column, length_f, inverse) + quarters)
        now = kept * cosine_of_turns(
            turns_of(number * (column + F32(LANES)), length_f, inverse) + quarters
        )
        first = jnp.broadcast_to(now[:, 0:1], now.shape)
        twice = F32(2.0) * jnp.where(odd, pltpu.roll(first, 1, axis=0), first)
        for block in range(points // LANES):
            value = before.astype(BF16)
            for third in range(THIRDS):
                phase[
                    pl.ds(pl.multiple_of(third * total_rows + step * tall, tall), tall),
                    block * LANES : (block + 1) * LANES,
                ] = value[third * tall : (third + 1) * tall, :]
            before, now = now, twice * now - before
        return carry

    lax.fori_loop(0, steps * 3 // 8, phase_rows, 0)

    whole_a = pltpu.make_async_copy(recv_a, recv_a, recv_sems.at[0])
    whole_a.wait()
    for source in range(levs):
        rows32[source * LANES : (source + 1) * LANES, 0:part] = recv_a[source].astype(F32).T
    for third in range(THIRDS):
        for side in range(2):
            start = third * PITCH + side
            block = jnp.concatenate(
                [
                    rows32[pl.ds(source * LANES + start, LEVEL_PITCH, stride=2), :]
                    for source in range(levs)
                ],
                axis=0,
            ).astype(BF16)
            product = jnp.dot(mixer[...], block, preferred_element_type=F32)
            for target in range(levs):
                turned[pl.ds(target * LANES + start, PITCH // 2, stride=2), :] = product[
                    target * LEVEL_PITCH : target * LEVEL_PITCH + PITCH // 2, :
                ]
    for target in range(levs):
        flipped = turned[target * LANES : (target + 1) * LANES, :].T[0:part, :]
        send_b[target] = flipped.astype(BF16).reshape(own_rows, ROWS, LANES)

    def place_b(k):
        target = lev_partner(high(k, own_rows), lev, levs)
        row = low(k, own_rows)
        return row, target, (lev * own_rows + row == wave) & (target == lev)

    def copy_b(row, target):
        return pltpu.make_async_remote_copy(
            src_ref=send_b.at[target, row],
            dst_ref=recv_b.at[wave],
            send_sem=send_sems.at[1],
            recv_sem=recv_sems.at[1],
            device_id=(lev * own_rows + row, target),
            device_id_type=MESH,
        )

    def start_b(k, carry):
        row, target, here = place_b(k)

        @pl.when(here)
        def _():
            pltpu.make_async_copy(
                send_b.at[target, row], recv_b.at[wave], recv_sems.at[1]
            ).start()

        @pl.when(jnp.logical_not(here))
        def _():
            copy_b(row, target).start()

        return carry

    @pl.when(core == 0)
    def _():
        pl.semaphore_wait(plane_sem, chips)

    if chips > 1:

        @pl.when(core == 1)
        def _():
            pl.semaphore_wait(plane_sem, chips - 1)

    lax.fori_loop(0, waves, start_b, 0)
    lax.fori_loop(steps * 3 // 8, steps, phase_rows, 0)

    chunk = 3 * LANES if points % (3 * LANES) == 0 else LANES
    pltpu.make_async_copy(recv_b, recv_b, recv_sems.at[1]).wait()
    received = recv_b[...].astype(F32).reshape(total_rows, LANES)
    for block in range(blocks):
        flipped = received[block * LANES : (block + 1) * LANES, :].T
        for third in range(THIRDS):
            at_lane = third * total_rows + block * LANES
            channels[:, at_lane : at_lane + LANES] = flipped[
                third * PITCH : (third + 1) * PITCH, :
            ].astype(BF16)
    for first in range(0, points, chunk):
        inside = first + lax.broadcasted_iota(jnp.int32, (CHANNELS, chunk), 1) < length
        grid = jnp.dot(
            channels[0:CHANNELS, :], phase[:, first : first + chunk], preferred_element_type=F32
        )
        grid = jnp.where(inside, grid, F32(0.0)).astype(BF16)
        grid_held[:, :, first : first + chunk] = grid.reshape(CHANNELS // 2, 2, chunk)
        added = forcing_in[:, :, first : first + chunk].reshape(CHANNELS, chunk).astype(F32)
        both = jnp.where(inside, grid.astype(F32) + added, F32(0.0))
        summed[:, first : first + chunk] = both.astype(BF16)
    store_grid = pltpu.make_async_copy(grid_held, grid_out, store_sems.at[0])
    store_grid.start()
    scale = quadrature_in[0] / length_f
    plane[...] = jnp.zeros_like(plane)

    def copy_c(target):
        return pltpu.make_async_remote_copy(
            src_ref=send_c.at[target],
            dst_ref=recv_c.at[wave],
            send_sem=send_sems.at[2],
            recv_sem=recv_sems.at[2],
            device_id=(target, lev),
            device_id_type=MESH,
        )

    for block in range(blocks):
        for third in range(THIRDS):
            first = third * total_rows + block * LANES
            back = lax.dot_general(
                summed[...], phase[first : first + LANES, :], NT_DIMS, preferred_element_type=F32
            )
            plane[third * PITCH : third * PITCH + CHANNELS, :] = back * scale
        send_c[block * block_waves : (block + 1) * block_waves] = (
            plane[...].T.astype(BF16).reshape(block_waves, ROWS, LANES)
        )

    def start_c(k, carry):
        copy_c(wave_partner(k, wave, waves)).start()
        return carry

    lax.fori_loop(0, waves - 1, start_c, 0)
    pltpu.make_async_copy(send_c.at[wave], recv_c.at[wave], recv_sems.at[2]).start()
    sent_a = send_a.at[pl.ds(0, (levs - 1) * part), :]
    pltpu.make_async_copy(sent_a, sent_a, send_sems.at[0]).wait()
    own_among = high(wave, own_rows) == lev

    def wait_sent(held, count, sem):
        sent = held.at[pl.ds(0, count)]
        pltpu.make_async_copy(sent, sent, sem).wait()

    @pl.when(own_among)
    def _():
        wait_sent(recv_b, waves - 1, send_sems.at[1])

    @pl.when(jnp.logical_not(own_among))
    def _():
        wait_sent(recv_b, waves, send_sems.at[1])

    wait_sent(send_c, waves - 1, send_sems.at[2])
    pltpu.make_async_copy(recv_c, recv_c, recv_sems.at[2]).wait()

    spread[0:total_rows, :] = recv_c[...].astype(F32).reshape(total_rows, LANES)
    for row in range(ROWS):
        turned[row * LANES : (row + 1) * LANES, 0:waves] = spread[
            pl.ds(row, waves, stride=ROWS), :
        ].T
    for s, third, group in slots_of():
        for part_at in range(2):
            base = (group * 2 + part_at) * LANES + third * PITCH
            north = turned[pl.ds(base, PITCH // 2, stride=2), :]
            south = turned[pl.ds(base + 1, PITCH // 2, stride=2), :]
            joined = jnp.concatenate([north[:, 0:waves], south[:, 0:waves]], axis=1)
            plane[pl.ds(part_at, PITCH // 2, stride=2), 0 : 2 * waves] = joined
        spectra_held[s] = jnp.dot(
            plane[0:CHANNELS, 0 : 2 * waves].astype(BF16), weights[s], preferred_element_type=F32
        ).astype(BF16).reshape(CHANNELS // 2, 2, degrees)
    store_spectra = pltpu.make_async_copy(spectra_held, spectra_out, store_sems.at[1])
    store_spectra.start()

    store_spectra.wait()
    store_grid.wait()


def hand_out(grid, spectra, grid_out, spectra_out, grid_held, spectra_held, sems):
    loads = [
        pltpu.make_async_copy(spectra, spectra_held, sems.at[0]),
        pltpu.make_async_copy(grid, grid_held, sems.at[1]),
    ]
    stores = [
        pltpu.make_async_copy(spectra_held, spectra_out, sems.at[2]),
        pltpu.make_async_copy(grid_held, grid_out, sems.at[3]),
    ]
    for load in loads:
        load.start()
    for load, store in zip(loads, stores):
        load.wait()
        store.start()
    for store in stores:
        store.wait()


def body(waves, levs, spectra, vertical, legendre, tile_mask, assign, row_points, quadrature, forcing):
    slots, fields, levels, parts, degrees = spectra.shape
    points = forcing.shape[-1]
    own_rows = waves // levs
    part = own_rows * ROWS
    total_rows = waves * ROWS
    hbm = pl.BlockSpec(memory_space=pl.ANY)
    turned_rows = max(levs, ROWS) * LANES
    grid, spectra_out = pl.pallas_call(
        functools.partial(kernel, waves, levs),
        out_shape=(
            jax.ShapeDtypeStruct((CHANNELS // 2, 2, points), BF16),
            jax.ShapeDtypeStruct((slots, CHANNELS // 2, 2, degrees), BF16),
        ),
        in_specs=[hbm] * 8,
        out_specs=(hbm, hbm),
        scratch_shapes=[
            pltpu.VMEM((slots, 2 * waves, degrees), BF16),
            pltpu.VMEM((levs * LEVEL_PITCH, levs * LEVEL_PITCH), BF16),
            pltpu.VMEM((THIRDS * total_rows, points), BF16),
            pltpu.VMEM((LANES, LANES), F32),
            pltpu.VMEM((levs * LANES + 8, LANES), F32),
            pltpu.VMEM((turned_rows, LANES), F32),
            pltpu.VMEM((total_rows + 8, LANES), F32),
            pltpu.VMEM((PITCH, THIRDS * total_rows), BF16),
            pltpu.VMEM((CHANNELS, points), BF16),
            pltpu.VMEM((total_rows, LANES), BF16),
            pltpu.VMEM((levs, part, LANES), BF16),
            pltpu.VMEM((levs, own_rows, ROWS, LANES), BF16),
            pltpu.VMEM((waves, ROWS, LANES), BF16),
            pltpu.VMEM((waves, ROWS, LANES), BF16),
            pltpu.VMEM((waves, ROWS, LANES), BF16),
            pltpu.VMEM((slots, CHANNELS // 2, 2, degrees), BF16),
            pltpu.VMEM(legendre.shape, BF16),
            pltpu.VMEM((CHANNELS // 2, 2, points), BF16),
            pltpu.VMEM(vertical.shape, BF16),
            pltpu.SMEM((slots, 1, tile_mask.shape[1]), jnp.int32),
            pltpu.SMEM(assign.shape, jnp.int32),
            pltpu.SMEM(row_points.shape, jnp.int32),
            pltpu.SMEM(quadrature.shape, F32),
            pltpu.VMEM((CHANNELS // 2, 2, points), BF16),
            pltpu.VMEM((slots, CHANNELS // 2, 2, degrees), BF16),
            pltpu.SemaphoreType.DMA((3,)),
            pltpu.SemaphoreType.DMA((3,)),
            pltpu.SemaphoreType.DMA((8,)),
            pltpu.SemaphoreType.DMA((2,)),
            pltpu.SemaphoreType.REGULAR,
            pltpu.SemaphoreType.REGULAR,
        ],
        compiler_params=pltpu.CompilerParams(
            collective_id=0, has_side_effects=True, vmem_limit_bytes=VMEM_BYTES
        ),
    )(
        spectra.reshape(slots, CHANNELS // 2, 2, degrees),
        legendre,
        jnp.transpose(tile_mask, (0, 2, 1)),
        assign,
        row_points,
        quadrature,
        vertical,
        forcing.reshape(CHANNELS // 2, 2, points),
    )
    grid, spectra_out = pl.pallas_call(
        hand_out,
        out_shape=(
            jax.ShapeDtypeStruct(grid.shape, BF16),
            jax.ShapeDtypeStruct(spectra_out.shape, BF16),
        ),
        in_specs=[hbm, hbm],
        out_specs=(hbm, hbm),
        scratch_shapes=[
            pltpu.VMEM(grid.shape, BF16),
            pltpu.VMEM(spectra_out.shape, BF16),
            pltpu.SemaphoreType.DMA((4,)),
        ],
        compiler_params=pltpu.CompilerParams(vmem_limit_bytes=VMEM_BYTES),
    )(grid, spectra_out)
    return grid.reshape(forcing.shape), spectra_out.reshape(spectra.shape)


def solution(mesh):
    return jax.shard_map(
        functools.partial(body, mesh.shape["wave"], mesh.shape["lev"]),
        mesh=mesh,
        in_specs=(
            P("wave", None, "lev", None, None),
            P(),
            P("wave", None, None),
            P("wave", None, None),
            P(),
            P("wave"),
            P("wave"),
            P(None, "lev", None, "wave", None),
        ),
        out_specs=(P(None, "lev", None, "wave", None), P("wave", None, "lev", None, None)),
        check_vma=False,
    )
```

```python
import functools
import math

import jax
import jax.numpy as jnp
from jax import lax
from jax.experimental import pallas as pl
from jax.experimental.pallas import tpu as pltpu
from jax.sharding import PartitionSpec as P

MESH = pl.DeviceIdType.MESH
F32 = jnp.float32
BF16 = jnp.bfloat16
LANES = 128
FIELDS = 3
OWN_LEVELS = 6
SLOTS = 10
GROUPS = 4
THIRDS = 3
PITCH = 40
LEVEL_PITCH = 24
ROWS = 2 * GROUPS
CHANNELS = 2 * FIELDS * OWN_LEVELS
STEP_WAVES = 4
VMEM_BYTES = 56 * 1024 * 1024
RING = 8
NT_DIMS = (((1,), (1,)), ((), ()))


def cosine_of_turns(turns):
    reduced = turns - jnp.round(turns)
    square = reduced * reduced
    terms = [(-1.0) ** k * (2.0 * math.pi) ** (2 * k) / math.factorial(2 * k) for k in range(9)]
    total = square * F32(terms[8]) + F32(terms[7])
    for term in terms[6::-1]:
        total = total * square + F32(term)
    return total


def turns_of(product, length, inverse):
    return (product - jnp.floor(product * inverse) * length) * inverse


def low(value, size):
    return value & (size - 1)


def high(value, size):
    return value >> (size.bit_length() - 1)


def far_first(index, size):
    step = (index + 1) >> 1
    return low(size // 2 + jnp.where((index & 1) == 0, step, -step), size)


def wave_partner(index, wave, waves):
    rows = waves // RING
    up = low(high(wave, RING) + far_first(high(index, RING), rows), rows)
    side = low(wave + far_first(low(index, RING), RING), RING)
    return up * RING + side


def lev_partner(index, lev, levs):
    chips = levs // 2
    chip = low((lev >> 1) + far_first(index >> 1, chips), chips)
    return chip * 2 + ((lev + index + 1) & 1)


def slots_of():
    return [(s, s // GROUPS, s % GROUPS) for s in range(SLOTS)]


def kernel(
    waves,
    levs,
    spectra,
    legendre,
    tiles,
    assign,
    row_points,
    quadrature,
    vertical,
    forcing,
    grid_out,
    spectra_out,
    weights,
    mixer,
    phase,
    plane,
    rows32,
    turned,
    spread,
    channels,
    summed,
    send_a,
    recv_a,
    send_b,
    recv_b,
    send_c,
    recv_c,
    spectra_in,
    legendre_in,
    forcing_in,
    vertical_in,
    tiles_in,
    assign_in,
    row_points_in,
    quadrature_in,
    grid_held,
    spectra_held,
    send_sems,
    recv_sems,
    load_sems,
    store_sems,
    line_sem,
    plane_sem,
):
    wave = lax.axis_index("wave")
    lev = lax.axis_index("lev")
    own_rows = waves // levs
    part = own_rows * ROWS
    total_rows = waves * ROWS
    degrees = spectra.shape[3]
    points = forcing.shape[2]
    block_waves = LANES // ROWS
    blocks = waves // block_waves

    pairs = (
        (assign, assign_in),
        (tiles, tiles_in),
        (legendre, legendre_in),
        (spectra, spectra_in),
        (vertical, vertical_in),
        (row_points, row_points_in),
        (quadrature, quadrature_in),
        (forcing, forcing_in),
    )
    loads = [
        pltpu.make_async_copy(source, held, load_sems.at[at])
        for at, (source, held) in enumerate(pairs)
    ]
    for load in loads:
        load.start()

    barrier = pltpu.get_barrier_semaphore()

    core = lev & 1
    chip = lev >> 1
    chips = levs // 2

    def greet(row, column):
        pl.semaphore_signal(barrier, inc=1, device_id=(row, column), device_id_type=MESH)

    def greet_plane(k, carry):
        greet(wave_partner(k, wave, waves), chip * 2 + 1)
        return carry

    def greet_line(k, carry):
        greet(wave, low(chip + far_first(k, chips), chips) * 2)
        return carry

    lax.fori_loop(0, chips - 1, greet_line, 0)
    greet(wave, lev + 1 - 2 * core)
    lax.fori_loop(0, waves - 1, greet_plane, 0)

    turned[...] = jnp.zeros_like(turned)
    plane[...] = jnp.zeros_like(plane)
    degree = lax.broadcasted_iota(jnp.int32, (1, degrees), 1)
    lane = lax.broadcasted_iota(jnp.int32, (1, LANES), 1)
    half = degrees // (2 * LANES // 2)
    for load in loads:
        load.wait()
    for s, third, group in slots_of():
        wave_number = assign_in[wave * SLOTS + s]
        marks = jnp.concatenate(
            [
                jnp.where(lane < LANES // 2, tiles_in[s, 0, 2 * k], tiles_in[s, 0, 2 * k + 1])
                for k in range(half)
            ],
            axis=1,
        )
        offset = degree - wave_number
        live = jnp.where((marks > 0) & (offset >= 0), F32(1.0), F32(0.0))
        signed = jnp.where((offset & 1) == 0, live, -live)
        table = legendre_in[s].astype(F32)
        lath = table.shape[0]
        weights[s, 0:lath, :] = (table * live).astype(BF16)
        weights[s, lath : 2 * lath, :] = (table * signed).astype(BF16)
        factor = jnp.where(wave_number == 0, F32(1.0), F32(2.0))
        plane[0:CHANNELS, 0 : 2 * lath] = factor * lax.dot_general(
            spectra_in[s].reshape(CHANNELS, degrees), weights[s], NT_DIMS, preferred_element_type=F32
        )
        for part_at in range(2):
            block = plane[pl.ds(part_at, PITCH // 2, stride=2), :]
            row = group * 2 + part_at
            base = row * LANES + third * PITCH
            turned[pl.ds(base, PITCH // 2, stride=2), :] = block
            turned[pl.ds(base + 1, PITCH // 2, stride=2), :] = pltpu.roll(
                block, LANES - lath, axis=1
            )
    for row in range(ROWS):
        flipped = turned[row * LANES : (row + 1) * LANES, :].T
        spread[pl.ds(row, waves, stride=ROWS), :] = flipped[0:waves, :]
    send_a[...] = spread[0:total_rows, :].astype(BF16)

    levels = vertical_in.shape[1]
    edge = levs * LEVEL_PITCH
    at_row = lax.broadcasted_iota(jnp.int32, (edge, levels), 0)
    at_level = lax.broadcasted_iota(jnp.int32, (edge, levels), 1)
    at_group = (at_row * 2731) >> 16
    at_inner = at_row - at_group * LEVEL_PITCH
    at_field = (at_inner * 43) >> 8
    wanted = at_group * OWN_LEVELS + at_inner - at_field * OWN_LEVELS
    mixed = jnp.zeros((edge, edge), F32)
    for field in range(FIELDS):
        pick = jnp.where((at_field == field) & (at_level == wanted), F32(1.0), F32(0.0)).astype(
            BF16
        )
        rows = jnp.dot(pick, vertical_in[field], preferred_element_type=F32).astype(BF16)
        mixed = mixed + lax.dot_general(rows, pick, NT_DIMS, preferred_element_type=F32)
    mixer[...] = mixed.astype(BF16)

    @pl.when(core == 0)
    def _():
        pl.semaphore_wait(barrier, levs - 1)
        pl.semaphore_signal(line_sem, inc=1, device_id=(wave, lev + 1), device_id_type=MESH)

    @pl.when(core == 1)
    def _():
        pl.semaphore_wait(line_sem, 1)

    def copy_a(target):
        return pltpu.make_async_remote_copy(
            src_ref=send_a.at[pl.ds(pl.multiple_of(target * part, part), part), :],
            dst_ref=recv_a.at[lev],
            send_sem=send_sems.at[0],
            recv_sem=recv_sems.at[0],
            device_id=(wave, target),
            device_id_type=MESH,
        )

    def start_a(k, carry):
        copy_a(lev_partner(k, lev, levs)).start()
        return carry

    lax.fori_loop(0, levs - 1, start_a, 0)
    own_a = pltpu.make_async_copy(
        send_a.at[pl.ds(pl.multiple_of(lev * part, part), part), :],
        recv_a.at[lev],
        recv_sems.at[0],
    )
    own_a.start()

    @pl.when(core == 1)
    def _():
        pl.semaphore_wait(barrier, 2 * waves - 1)

        def tell(k, carry):
            pl.semaphore_signal(
                plane_sem,
                inc=1,
                device_id=(wave, lev_partner(k, lev, levs)),
                device_id_type=MESH,
            )
            return carry

        lax.fori_loop(0, levs - 1, tell, 0)

    length = row_points_in[0]
    length_f = length.astype(F32)
    inverse = F32(1.0) / length_f
    tall = STEP_WAVES * ROWS
    at = lax.broadcasted_iota(jnp.int32, (tall, LANES), 0)
    at_pair = at >> 1
    odd = jnp.concatenate([(at & 1) == 1] * THIRDS, axis=0)
    quarters = jnp.where(odd, F32(0.25), F32(0.0))
    column = lax.broadcasted_iota(jnp.int32, (THIRDS * tall, LANES), 1).astype(F32)
    group_at = at_pair & (GROUPS - 1)
    real = jnp.concatenate(
        [jnp.where(group_at < SLOTS - third * GROUPS, F32(1.0), F32(0.0)) for third in range(THIRDS)],
        axis=0,
    )
    steps = waves // STEP_WAVES

    def phase_rows(step, carry):
        numbers = []
        for third in range(THIRDS):
            number = jnp.zeros((tall, LANES), jnp.int32)
            for near in range(STEP_WAVES):
                for group in range(GROUPS):
                    s = third * GROUPS + group
                    if s < SLOTS:
                        held = assign_in[(step * STEP_WAVES + near) * SLOTS + s]
                        number = jnp.where(at_pair == near * GROUPS + group, held, number)
            numbers.append(number)
        number = jnp.concatenate(numbers, axis=0)
        kept = jnp.where(2 * number < length, real, F32(0.0))
        number = number.astype(F32)
        before = kept * cosine_of_turns(turns_of(number * column, length_f, inverse) + quarters)
        now = kept * cosine_of_turns(
            turns_of(number * (column + F32(LANES)), length_f, inverse) + quarters
        )
        first = jnp.broadcast_to(now[:, 0:1], now.shape)
        twice = F32(2.0) * jnp.where(odd, pltpu.roll(first, 1, axis=0), first)
        for block in range(points // LANES):
            value = before.astype(BF16)
            for third in range(THIRDS):
                phase[
                    pl.ds(pl.multiple_of(third * total_rows + step * tall, tall), tall),
                    block * LANES : (block + 1) * LANES,
                ] = value[third * tall : (third + 1) * tall, :]
            before, now = now, twice * now - before
        return carry

    lax.fori_loop(0, steps * 3 // 8, phase_rows, 0)

    whole_a = pltpu.make_async_copy(recv_a, recv_a, recv_sems.at[0])
    whole_a.wait()
    for source in range(levs):
        rows32[source * LANES : (source + 1) * LANES, 0:part] = recv_a[source].astype(F32).T
    for third in range(THIRDS):
        for side in range(2):
            start = third * PITCH + side
            block = jnp.concatenate(
                [
                    rows32[pl.ds(source * LANES + start, LEVEL_PITCH, stride=2), :]
                    for source in range(levs)
                ],
                axis=0,
            ).astype(BF16)
            product = jnp.dot(mixer[...], block, preferred_element_type=F32)
            for target in range(levs):
                turned[pl.ds(target * LANES + start, PITCH // 2, stride=2), :] = product[
                    target * LEVEL_PITCH : target * LEVEL_PITCH + PITCH // 2, :
                ]
    for target in range(levs):
        flipped = turned[target * LANES : (target + 1) * LANES, :].T[0:part, :]
        send_b[target] = flipped.astype(BF16).reshape(own_rows, ROWS, LANES)

    def place_b(k):
        target = lev_partner(high(k, own_rows), lev, levs)
        row = low(k, own_rows)
        return row, target, (lev * own_rows + row == wave) & (target == lev)

    def copy_b(row, target):
        return pltpu.make_async_remote_copy(
            src_ref=send_b.at[target, row],
            dst_ref=recv_b.at[wave],
            send_sem=send_sems.at[1],
            recv_sem=recv_sems.at[1],
            device_id=(lev * own_rows + row, target),
            device_id_type=MESH,
        )

    def start_b(k, carry):
        row, target, here = place_b(k)

        @pl.when(here)
        def _():
            pltpu.make_async_copy(
                send_b.at[target, row], recv_b.at[wave], recv_sems.at[1]
            ).start()

        @pl.when(jnp.logical_not(here))
        def _():
            copy_b(row, target).start()

        return carry

    @pl.when(core == 0)
    def _():
        pl.semaphore_wait(plane_sem, chips)

    if chips > 1:

        @pl.when(core == 1)
        def _():
            pl.semaphore_wait(plane_sem, chips - 1)

    lax.fori_loop(0, waves, start_b, 0)
    lax.fori_loop(steps * 3 // 8, steps, phase_rows, 0)

    chunk = 3 * LANES if points % (3 * LANES) == 0 else LANES
    pltpu.make_async_copy(recv_b, recv_b, recv_sems.at[1]).wait()
    received = recv_b[...].astype(F32).reshape(total_rows, LANES)
    for block in range(blocks):
        flipped = received[block * LANES : (block + 1) * LANES, :].T
        for third in range(THIRDS):
            at_lane = third * total_rows + block * LANES
            channels[:, at_lane : at_lane + LANES] = flipped[
                third * PITCH : (third + 1) * PITCH, :
            ].astype(BF16)
    for first in range(0, points, chunk):
        inside = first + lax.broadcasted_iota(jnp.int32, (CHANNELS, chunk), 1) < length
        grid = jnp.dot(
            channels[0:CHANNELS, :], phase[:, first : first + chunk], preferred_element_type=F32
        )
        grid = jnp.where(inside, grid, F32(0.0)).astype(BF16)
        grid_held[:, :, first : first + chunk] = grid.reshape(CHANNELS // 2, 2, chunk)
        added = forcing_in[:, :, first : first + chunk].reshape(CHANNELS, chunk).astype(F32)
        both = jnp.where(inside, grid.astype(F32) + added, F32(0.0))
        summed[:, first : first + chunk] = both.astype(BF16)
    store_grid = pltpu.make_async_copy(grid_held, grid_out, store_sems.at[0])
    store_grid.start()
    scale = quadrature_in[0] / length_f
    plane[...] = jnp.zeros_like(plane)

    def copy_c(target):
        return pltpu.make_async_remote_copy(
            src_ref=send_c.at[target],
            dst_ref=recv_c.at[wave],
            send_sem=send_sems.at[2],
            recv_sem=recv_sems.at[2],
            device_id=(target, lev),
            device_id_type=MESH,
        )

    for block in range(blocks):
        for third in range(THIRDS):
            first = third * total_rows + block * LANES
            back = lax.dot_general(
                summed[...], phase[first : first + LANES, :], NT_DIMS, preferred_element_type=F32
            )
            plane[third * PITCH : third * PITCH + CHANNELS, :] = back * scale
        send_c[block * block_waves : (block + 1) * block_waves] = (
            plane[...].T.astype(BF16).reshape(block_waves, ROWS, LANES)
        )

    def start_c(k, carry):
        copy_c(wave_partner(k, wave, waves)).start()
        return carry

    lax.fori_loop(0, waves - 1, start_c, 0)
    pltpu.make_async_copy(send_c.at[wave], recv_c.at[wave], recv_sems.at[2]).start()
    sent_a = send_a.at[pl.ds(0, (levs - 1) * part), :]
    pltpu.make_async_copy(sent_a, sent_a, send_sems.at[0]).wait()
    own_among = high(wave, own_rows) == lev

    def wait_sent(held, count, sem):
        sent = held.at[pl.ds(0, count)]
        pltpu.make_async_copy(sent, sent, sem).wait()

    @pl.when(own_among)
    def _():
        wait_sent(recv_b, waves - 1, send_sems.at[1])

    @pl.when(jnp.logical_not(own_among))
    def _():
        wait_sent(recv_b, waves, send_sems.at[1])

    pltpu.make_async_copy(recv_c, recv_c, recv_sems.at[2]).wait()

    spread[0:total_rows, :] = recv_c[...].astype(F32).reshape(total_rows, LANES)
    for row in range(ROWS):
        turned[row * LANES : (row + 1) * LANES, 0:waves] = spread[
            pl.ds(row, waves, stride=ROWS), :
        ].T
    for s, third, group in slots_of():
        for part_at in range(2):
            base = (group * 2 + part_at) * LANES + third * PITCH
            north = turned[pl.ds(base, PITCH // 2, stride=2), :]
            south = turned[pl.ds(base + 1, PITCH // 2, stride=2), :]
            joined = jnp.concatenate([north[:, 0:waves], south[:, 0:waves]], axis=1)
            plane[pl.ds(part_at, PITCH // 2, stride=2), 0 : 2 * waves] = joined
        spectra_held[s] = jnp.dot(
            plane[0:CHANNELS, 0 : 2 * waves].astype(BF16), weights[s], preferred_element_type=F32
        ).astype(BF16).reshape(CHANNELS // 2, 2, degrees)
    store_spectra = pltpu.make_async_copy(spectra_held, spectra_out, store_sems.at[1])
    store_spectra.start()

    wait_sent(send_c, waves - 1, send_sems.at[2])
    store_spectra.wait()
    store_grid.wait()


def hand_out(grid, spectra, grid_out, spectra_out, grid_held, spectra_held, sems):
    loads = [
        pltpu.make_async_copy(spectra, spectra_held, sems.at[0]),
        pltpu.make_async_copy(grid, grid_held, sems.at[1]),
    ]
    stores = [
        pltpu.make_async_copy(spectra_held, spectra_out, sems.at[2]),
        pltpu.make_async_copy(grid_held, grid_out, sems.at[3]),
    ]
    for load in loads:
        load.start()
    for load, store in zip(loads, stores):
        load.wait()
        store.start()
    for store in stores:
        store.wait()


def body(waves, levs, spectra, vertical, legendre, tile_mask, assign, row_points, quadrature, forcing):
    slots, fields, levels, parts, degrees = spectra.shape
    points = forcing.shape[-1]
    own_rows = waves // levs
    part = own_rows * ROWS
    total_rows = waves * ROWS
    hbm = pl.BlockSpec(memory_space=pl.ANY)
    turned_rows = max(levs, ROWS) * LANES
    grid, spectra_out = pl.pallas_call(
        functools.partial(kernel, waves, levs),
        out_shape=(
            jax.ShapeDtypeStruct((CHANNELS // 2, 2, points), BF16),
            jax.ShapeDtypeStruct((slots, CHANNELS // 2, 2, degrees), BF16),
        ),
        in_specs=[hbm] * 8,
        out_specs=(hbm, hbm),
        scratch_shapes=[
            pltpu.VMEM((slots, 2 * waves, degrees), BF16),
            pltpu.VMEM((levs * LEVEL_PITCH, levs * LEVEL_PITCH), BF16),
            pltpu.VMEM((THIRDS * total_rows, points), BF16),
            pltpu.VMEM((LANES, LANES), F32),
            pltpu.VMEM((levs * LANES + 8, LANES), F32),
            pltpu.VMEM((turned_rows, LANES), F32),
            pltpu.VMEM((total_rows + 8, LANES), F32),
            pltpu.VMEM((PITCH, THIRDS * total_rows), BF16),
            pltpu.VMEM((CHANNELS, points), BF16),
            pltpu.VMEM((total_rows, LANES), BF16),
            pltpu.VMEM((levs, part, LANES), BF16),
            pltpu.VMEM((levs, own_rows, ROWS, LANES), BF16),
            pltpu.VMEM((waves, ROWS, LANES), BF16),
            pltpu.VMEM((waves, ROWS, LANES), BF16),
            pltpu.VMEM((waves, ROWS, LANES), BF16),
            pltpu.VMEM((slots, CHANNELS // 2, 2, degrees), BF16),
            pltpu.VMEM(legendre.shape, BF16),
            pltpu.VMEM((CHANNELS // 2, 2, points), BF16),
            pltpu.VMEM(vertical.shape, BF16),
            pltpu.SMEM((slots, 1, tile_mask.shape[1]), jnp.int32),
            pltpu.SMEM(assign.shape, jnp.int32),
            pltpu.SMEM(row_points.shape, jnp.int32),
            pltpu.SMEM(quadrature.shape, F32),
            pltpu.VMEM((CHANNELS // 2, 2, points), BF16),
            pltpu.VMEM((slots, CHANNELS // 2, 2, degrees), BF16),
            pltpu.SemaphoreType.DMA((3,)),
            pltpu.SemaphoreType.DMA((3,)),
            pltpu.SemaphoreType.DMA((8,)),
            pltpu.SemaphoreType.DMA((2,)),
            pltpu.SemaphoreType.REGULAR,
            pltpu.SemaphoreType.REGULAR,
        ],
        compiler_params=pltpu.CompilerParams(
            collective_id=0, has_side_effects=True, vmem_limit_bytes=VMEM_BYTES
        ),
    )(
        spectra.reshape(slots, CHANNELS // 2, 2, degrees),
        legendre,
        jnp.transpose(tile_mask, (0, 2, 1)),
        assign,
        row_points,
        quadrature,
        vertical,
        forcing.reshape(CHANNELS // 2, 2, points),
    )
    grid, spectra_out = pl.pallas_call(
        hand_out,
        out_shape=(
            jax.ShapeDtypeStruct(grid.shape, BF16),
            jax.ShapeDtypeStruct(spectra_out.shape, BF16),
        ),
        in_specs=[hbm, hbm],
        out_specs=(hbm, hbm),
        scratch_shapes=[
            pltpu.VMEM(grid.shape, BF16),
            pltpu.VMEM(spectra_out.shape, BF16),
            pltpu.SemaphoreType.DMA((4,)),
        ],
        compiler_params=pltpu.CompilerParams(vmem_limit_bytes=VMEM_BYTES),
    )(grid, spectra_out)
    return grid.reshape(forcing.shape), spectra_out.reshape(spectra.shape)


def solution(mesh):
    return jax.shard_map(
        functools.partial(body, mesh.shape["wave"], mesh.shape["lev"]),
        mesh=mesh,
        in_specs=(
            P("wave", None, "lev", None, None),
            P(),
            P("wave", None, None),
            P("wave", None, None),
            P(),
            P("wave"),
            P("wave"),
            P(None, "lev", None, "wave", None),
        ),
        out_specs=(P(None, "lev", None, "wave", None), P("wave", None, "lev", None, None)),
        check_vma=False,
    )
```
